256 devices in a mesh: row: 8 (over x_hi, y), col: 32 (over x_lo, z, core).
Axes of the slice: x: 4 (x_hi: 2, x_lo: 2; x = x_hi * 2 + x_lo), y: 4, z: 8, core: 2. Of those that a mesh axis runs over, the one named last changes fastest.
Arguments:
- pair: bfloat16 [768, 768, 128], P('row', 'col'), may hold values from -1.5 to 1.5
- norm_gain: float32 [2, 128], replicated, may hold values from 0.1 to 1.9
- w_proj: bfloat16 [2, 128, 512], replicated, may hold values from -5 to 5
- w_bias: bfloat16 [2, 128, 4], replicated, may hold values from -1 to 1
- gate_bias: float32 [2, 128], replicated, may hold values from -4 to 4
- w_out: bfloat16 [2, 128, 128], replicated, may hold values from -1 to 1
- out_bias: float32 [2, 128], replicated, may hold values from -3 to 3
Outputs:
- updated_pair: bfloat16 [768, 768, 128], P('row', 'col')
The draws below stay inside these ranges and needn't reach their ends.
All inputs are finite; a program needn't handle non-finite values.
Results may differ from the reference program's by a relative error of at most 0.03.
Values may be sent and summed in bfloat16 or wider, within the bound.
No kernel may reach another device: no remote copies, remote signals or barrier semaphores. Data moves between devices by JAX's collectives and lax.ppermute only.
A program may use at most 64 MiB of HBM per device.

```python
import jax
import jax.numpy as jnp
from jax import lax

RESIDUES = 768
CHANNELS = 128
HEAD_COUNT = 4
HEAD_WIDTH = 32


def shared_directions(key):
    return jnp.clip(jax.random.normal(key, (2, CHANNELS, HEAD_COUNT), jnp.float32), -4.0, 4.0)


def draw_pair(key, part):
    key = jax.random.fold_in(key, 11)
    key_noise, key_column, key_row = jax.random.split(key, 3)
    noise = jnp.clip(jax.random.normal(key_noise, (RESIDUES, RESIDUES, CHANNELS), jnp.float32), -4.0, 4.0)
    column_part = jnp.clip(jax.random.normal(key_column, (RESIDUES, CHANNELS), jnp.float32), -4.0, 4.0)
    row_part = jnp.clip(jax.random.normal(key_row, (RESIDUES, CHANNELS), jnp.float32), -4.0, 4.0)
    mixed = 0.55 * noise + 0.6 * column_part[None, :, :] + 0.55 * row_part[:, None, :]
    return jnp.clip(0.25 * mixed, -1.5, 1.5).astype(jnp.bfloat16)


def draw_w_bias(key, part):
    directions = shared_directions(key)
    return (directions * (1.25 * CHANNELS ** (-0.5))).astype(jnp.bfloat16)


def draw_w_proj(key, part):
    directions = shared_directions(key)
    key = jax.random.fold_in(key, 7)
    key_base, key_sign = jax.random.split(key)
    inner = HEAD_COUNT * HEAD_WIDTH
    base = jax.random.truncated_normal(key_base, -6.0, 6.0, (2, CHANNELS, 4 * inner), jnp.float32) * CHANNELS ** (-0.5)
    column_scale = jnp.where(jnp.arange(4 * inner) < 2 * inner, 0.7, 1.0).astype(jnp.float32)
    base = base * column_scale[None, None, :]
    signs = jnp.where(jax.random.bernoulli(key_sign, 0.5, (2, inner)), 1.0, -1.0).astype(jnp.float32)
    head_of = jnp.arange(inner) // HEAD_WIDTH
    value_lift = 1.8 * CHANNELS ** (-0.5) * directions[:, :, head_of] * signs[:, None, :]
    base = base.at[:, :, 2 * inner:3 * inner].add(value_lift)
    return base.astype(jnp.bfloat16)


def gaussian(key, extent, deviation, bound, dtype=jnp.bfloat16):
    values = deviation * jax.random.normal(key, extent, jnp.float32)
    return jnp.clip(values, min=-bound, max=bound).astype(dtype)


def setup_inputs(seed: int = 0) -> dict:
    streams_of = jax.random.split(jax.random.key(seed), 8)
    return {
        "pair": draw_pair(jax.random.fold_in(streams_of[7], 71), 0),
        "norm_gain": jnp.clip(1.0 + 0.18 * jax.random.normal(streams_of[1], (2, CHANNELS), jnp.float32), 0.1, 1.9),
        "w_proj": draw_w_proj(jax.random.fold_in(streams_of[7], 71), 0),
        "w_bias": draw_w_bias(jax.random.fold_in(streams_of[7], 71), 0),
        "gate_bias": gaussian(streams_of[4], (2, HEAD_COUNT * HEAD_WIDTH), 1.0, 4.0, jnp.float32),
        "w_out": gaussian(streams_of[5], (2, HEAD_COUNT * HEAD_WIDTH, CHANNELS), HEAD_WIDTH ** -0.5, 1.0),
        "out_bias": gaussian(streams_of[6], (2, CHANNELS), 0.5, 3.0, jnp.float32),
    }


def normalize(pair_map, gain):
    values = pair_map.astype(jnp.float32)
    center = lax.optimization_barrier(jnp.mean(values, axis=-1, keepdims=True))
    spread = lax.optimization_barrier(jnp.mean((values - center) ** 2, axis=-1, keepdims=True))
    return ((values - center) * lax.rsqrt(spread + 1e-05) * gain).astype(jnp.bfloat16)

def update(pair_map, gain, proj_weight, bias_weight, gate_shift, out_weight, out_shift):
    inner = HEAD_COUNT * HEAD_WIDTH
    normed = normalize(pair_map, gain)
    pair_bias = jnp.einsum('abc,ch->hab', normed.astype(jnp.float32), bias_weight.astype(jnp.float32)).astype(jnp.bfloat16)
    scale = HEAD_WIDTH ** (-0.5)

    def one_row(row_entries):
        projected = jnp.dot(row_entries, proj_weight, preferred_element_type=jnp.float32)
        queries = projected[:, :inner].astype(jnp.bfloat16).reshape(RESIDUES, HEAD_COUNT, HEAD_WIDTH)
        key_rows = projected[:, inner:2 * inner].astype(jnp.bfloat16).reshape(RESIDUES, HEAD_COUNT, HEAD_WIDTH)
        value_rows = projected[:, 2 * inner:3 * inner].astype(jnp.bfloat16).reshape(RESIDUES, HEAD_COUNT, HEAD_WIDTH)
        scores = jnp.einsum('jhd,khd->hjk', queries.astype(jnp.float32), key_rows.astype(jnp.float32)) * scale + pair_bias.astype(jnp.float32)
        weights = jax.nn.softmax(scores, axis=-1).astype(jnp.bfloat16)
        mixed = jnp.einsum('hjk,khd->jhd', weights.astype(jnp.float32), value_rows.astype(jnp.float32)).reshape(RESIDUES, inner)
        gated = (mixed * jax.nn.sigmoid(projected[:, 3 * inner:] + gate_shift)).astype(jnp.bfloat16)
        return jnp.dot(gated, out_weight, preferred_element_type=jnp.float32) + out_shift
    return lax.map(one_row, normed)

def reference(pair, norm_gain, w_proj, w_bias, gate_bias, w_out, out_bias):
    first_delta = update(pair, norm_gain[0], w_proj[0], w_bias[0], gate_bias[0], w_out[0], out_bias[0])
    first = (pair.astype(jnp.float32) + first_delta).astype(jnp.bfloat16)
    flipped = jnp.swapaxes(first, 0, 1)
    second_delta = update(flipped, norm_gain[1], w_proj[1], w_bias[1], gate_bias[1], w_out[1], out_bias[1])
    return (first.astype(jnp.float32) + jnp.swapaxes(second_delta, 0, 1)).astype(jnp.bfloat16)
```

```python
import functools

import jax
import jax.numpy as jnp
from jax import lax
from jax.experimental import pallas as pl
from jax.experimental.pallas import tpu as pltpu
from jax.sharding import PartitionSpec as P

HEADS = 4
WIDTH = 32
CH = 128
LOG2E = 1.4426950408889634
NT = (((1,), (1,)), ((), ()))


def normalize(values, gain):
    values = values.astype(jnp.float32)
    center = jnp.mean(values, axis=-1, keepdims=True)
    spread = jnp.mean((values - center) ** 2, axis=-1, keepdims=True)
    return ((values - center) * lax.rsqrt(spread + 1e-05) * gain).astype(jnp.bfloat16)


def attention_kernel(
    nblk, blk_ref, x_ref, xq_ref, *refs
):
    bias_refs = refs[:nblk]
    gain_ref, wp_ref, gb_ref, wo_ref, ob_ref, out_ref, biasf = refs[nblk:]
    keys = x_ref.shape[1]
    half = bias_refs[0].shape[0]
    rows = bias_refs[0].shape[1] // 2
    block = rows // HEADS

    @pl.when(pl.program_id(0) == 0)
    def _():
        at = lax.broadcasted_iota(jnp.int32, (rows, 2 * rows), 0)
        to = lax.broadcasted_iota(jnp.int32, (rows, 2 * rows), 1)
        for s in range(2):
            pick = (to == at + s * rows).astype(jnp.bfloat16)
            for b in range(nblk):
                biasf[b, :, s * half : (s + 1) * half] = (
                    lax.dot_general(pick, bias_refs[b][...], NT, preferred_element_type=jnp.float32)
                    * LOG2E
                )

    gain = gain_ref[...]
    xn = normalize(x_ref[0], gain)
    kv = jnp.dot(xn, wp_ref[:, CH : 3 * CH], preferred_element_type=jnp.float32).astype(jnp.bfloat16)
    k2 = jnp.concatenate([kv[:, :CH], kv[:, :CH]], axis=1)
    v1 = jnp.concatenate([kv[:, CH:], jnp.ones((keys, CH), jnp.bfloat16)], axis=1)
    head_of = lax.broadcasted_iota(jnp.int32, (block, CH), 1) // WIDTH

    for b in range(nblk):
        q0 = pl.multiple_of(blk_ref[b] * block, 16)
        xq = xq_ref[0, pl.ds(q0, block), :]
        xqn = normalize(xq, gain)
        q = jnp.dot(xqn, wp_ref[:, :CH], preferred_element_type=jnp.float32)
        gate = jnp.dot(xqn, wp_ref[:, 3 * CH :], preferred_element_type=jnp.float32)
        qs = q.astype(jnp.bfloat16).astype(jnp.float32) * (WIDTH**-0.5 * LOG2E)
        qh = qs.astype(jnp.bfloat16).astype(jnp.float32)
        ql = qs - qh
        qm = jnp.concatenate(
            [
                jnp.concatenate([jnp.where(head_of == h, t, 0.0) for t in (qh, ql)], axis=1)
                for h in range(HEADS)
            ],
            axis=0,
        ).astype(jnp.bfloat16)
        s = lax.dot_general(qm, k2, NT, preferred_element_type=jnp.float32) + biasf[b]
        top = jnp.max(s, axis=-1, keepdims=True)
        p = jnp.exp2(s - top).astype(jnp.bfloat16)
        o = jnp.dot(p, v1, preferred_element_type=jnp.float32)
        o = o[:, :CH] / o[:, CH:]
        mixed = jnp.zeros((block, CH), jnp.float32)
        for h in range(HEADS):
            mixed = jnp.where(head_of == h, o[h * block : (h + 1) * block], mixed)
        gated = (mixed * jax.nn.sigmoid(gate + gb_ref[...])).astype(jnp.bfloat16)
        y = jnp.dot(gated, wo_ref[...], preferred_element_type=jnp.float32) + ob_ref[...]
        out_ref[0, pl.ds(q0, block), :] = (xq.astype(jnp.float32) + y).astype(jnp.bfloat16)


def attention(blocks, x, xq, biases, gain, wp, gb, wo, ob):
    nrow, keys, _ = x.shape
    nq = xq.shape[1]
    nblk = len(biases)
    rows = biases[0].shape[1] // 2
    whole = lambda a: pl.BlockSpec(a.shape, lambda i, *_: (0,) * a.ndim)
    small = [gain[None], wp, gb[None], wo, ob[None]]
    flops = 2 * nrow * HEADS * nq * keys * 512
    return pl.pallas_call(
        functools.partial(attention_kernel, nblk),
        grid_spec=pltpu.PrefetchScalarGridSpec(
            num_scalar_prefetch=1,
            grid=(nrow,),
            in_specs=[
                pl.BlockSpec((1, keys, CH), lambda i, *_: (i, 0, 0)),
                pl.BlockSpec((1, nq, CH), lambda i, *_: (i, 0, 0)),
            ]
            + [whole(a) for a in list(biases) + small],
            out_specs=pl.BlockSpec((1, nq, CH), lambda i, *_: (i, 0, 0)),
            scratch_shapes=[pltpu.VMEM((nblk, rows, keys), jnp.float32)],
        ),
        out_shape=jax.ShapeDtypeStruct((nrow, nq, CH), jnp.bfloat16),
        compiler_params=pltpu.CompilerParams(vmem_limit_bytes=40 << 20),
        cost_estimate=pl.CostEstimate(
            flops=flops, bytes_accessed=6 << 20, transcendentals=nrow * HEADS * nq * keys
        ),
    )(blocks, x, xq, *biases, *small)


def solution(mesh):
    nr, nc = mesh.shape["row"], mesh.shape["col"]
    ng = nc // 2
    same_core_col = [[2 * g + c for g in range(ng)] for c in range(2)]
    same_core_all = [[r * nc + 2 * g + c for r in range(nr) for g in range(ng)] for c in range(2)]
    swap_core = [(i, i ^ 1) for i in range(nc)]
    turns = ((0, 1), (0, 3), (1, 0), (0, 2), (1, 1), (1, 3), (1, 2))

    def turned(i, dx, dy):
        return ((i // 4) ^ dx) * 4 + (i % 4 + dy) % 4

    def spread(bias):
        me = lax.axis_index("row")
        got, ids = [bias], [me]
        for dx, dy in turns:
            got.append(lax.ppermute(bias, "row", [(i, turned(i, dx, dy)) for i in range(nr)]))
            ids.append(((me // 4) ^ dx) * 4 + (me % 4 - dy + 4) % 4)
        return got, jnp.stack(ids).astype(jnp.int32)

    def per_device(pair, norm_gain, w_proj, w_bias, gate_bias, w_out, out_bias):
        core = lax.axis_index("col") % 2
        nrow = pair.shape[0] // ng
        ncol = pair.shape[1]
        keys = nc * ncol
        half = keys // 2
        normed = normalize(pair, norm_gain[0])
        local = jnp.einsum("qmc,ch->mhq", normed, w_bias[0], preferred_element_type=jnp.float32)
        local = local.astype(jnp.bfloat16).reshape(ncol, HEADS, 2, 2, ncol).transpose(0, 3, 1, 2, 4)
        local = jnp.where(core == 0, local, local[:, ::-1]).reshape(-1, CH)
        brow = local.shape[0]
        message = jnp.concatenate(
            [
                pair.reshape(ng, nrow * ncol, CH),
                jnp.broadcast_to(local[None], (ng, brow, CH)),
                jnp.zeros((ng, -brow % 16, CH), jnp.bfloat16),
            ],
            axis=1,
        )
        got = lax.all_to_all(message, "col", 0, 0, tiled=True, axis_index_groups=same_core_col)
        x_own = got[:, : nrow * ncol]
        x_other = lax.ppermute(x_own, "col", swap_core)
        bias = got[:, nrow * ncol : nrow * ncol + brow].reshape(half, 2, half // 2)
        bias_other = lax.ppermute(bias[:, 1], "col", swap_core)
        bias = jnp.concatenate([bias[:, 0], bias_other], axis=1)
        biases, ids = spread(bias)
        x = jnp.stack([x_own, x_other]).reshape(2, ng, nrow, ncol, CH)
        x = x.transpose(2, 0, 1, 3, 4).reshape(nrow, keys, CH)
        first = attention(
            ids, x, x[:, :half], biases, norm_gain[0], w_proj[0], gate_bias[0], w_out[0], out_bias[0]
        )

        part = ncol // nr
        moved = first.reshape(nrow, ng, nr, part, CH).transpose(2, 1, 0, 3, 4)
        moved = moved.reshape(nr, ng, nrow * part, CH)
        normed = normalize(first, norm_gain[1])
        local = jnp.einsum("mqc,ch->mhq", normed, w_bias[1], preferred_element_type=jnp.float32)
        local = local.astype(jnp.bfloat16).reshape(nrow, HEADS, nr, half // nr).transpose(2, 0, 1, 3)
        local = local.reshape(nr, 1, -1, CH)
        brow = local.shape[2]
        message = jnp.concatenate(
            [
                moved,
                jnp.broadcast_to(local, (nr, ng, brow, CH)),
                jnp.zeros((nr, ng, -(brow + nrow * part) % 16, CH), jnp.bfloat16),
            ],
            axis=2,
        ).reshape(nr * ng, -1, CH)
        got = lax.all_to_all(
            message, ("row", "col"), 0, 0, tiled=True, axis_index_groups=same_core_all
        )
        x_own = got[:, : nrow * part].reshape(keys, part, CH).transpose(1, 0, 2)
        x_other = lax.ppermute(x_own, "col", swap_core)
        bias = got[:, nrow * part : nrow * part + brow].reshape(2, half, half // 2)
        bias = jnp.concatenate([bias[0], bias[1]], axis=1)
        biases, ids = spread(bias)
        x = jnp.concatenate([x_own, x_other])
        xq = x.reshape(2 * part, ng, 2, ncol, CH)
        xq = jnp.where(core == 0, xq[:, :, 0], xq[:, :, 1]).reshape(2 * part, half, CH)
        last = attention(
            ids, x, xq, biases, norm_gain[1], w_proj[1], gate_bias[1], w_out[1], out_bias[1]
        )

        own = last[:part]
        other = lax.ppermute(last[part:], "col", swap_core)
        both = jnp.stack([jnp.where(core == 0, own, other), jnp.where(core == 0, other, own)])
        both = both.reshape(2, part, nr, half // nr, CH).transpose(2, 0, 1, 3, 4)
        got = lax.all_to_all(both.reshape(nr, -1, CH), "row", 0, 0, tiled=True)
        got = got.reshape(nr, 2, part, 2, ncol, CH)
        return got.transpose(3, 1, 4, 0, 2, 5).reshape(pair.shape)

    return jax.shard_map(
        per_device,
        mesh=mesh,
        in_specs=(P("row", "col", None), P(), P(), P(), P(), P(), P()),
        out_specs=P("row", "col", None),
        check_vma=False,
    )
```

```python
import functools

import jax
import jax.numpy as jnp
from jax import lax
from jax.experimental import pallas as pl
from jax.experimental.pallas import tpu as pltpu
from jax.sharding import PartitionSpec as P

HEADS = 4
WIDTH = 32
CH = 128
LOG2E = 1.4426950408889634
CALLS = (4, 4)
NT = (((1,), (1,)), ((), ()))


def normalize(values, gain):
    values = values.astype(jnp.float32)
    center = jnp.mean(values, axis=-1, keepdims=True)
    spread = jnp.mean((values - center) ** 2, axis=-1, keepdims=True)
    return ((values - center) * lax.rsqrt(spread + 1e-05) * gain).astype(jnp.bfloat16)


def whole(a):
    return pl.BlockSpec(a.shape, lambda i, *_: (0,) * a.ndim)


def by_row(a):
    return pl.BlockSpec((1,) + a.shape[1:], lambda i, *_: (i, 0, 0))


def prepare_kernel(x_ref, xq_ref, gain_ref, wp_ref, gb_ref, kt_ref, v_ref, q_ref, gate_ref):
    gain = gain_ref[...]
    xn = normalize(x_ref[0], gain)
    k = jnp.dot(xn, wp_ref[:, CH : 2 * CH], preferred_element_type=jnp.float32)
    kt_ref[0] = k.astype(jnp.bfloat16).T
    v = jnp.dot(xn, wp_ref[:, 2 * CH : 3 * CH], preferred_element_type=jnp.float32)
    v_ref[0] = v.astype(jnp.bfloat16)
    xqn = normalize(xq_ref[0], gain)
    q = jnp.dot(xqn, wp_ref[:, :CH], preferred_element_type=jnp.float32)
    q_ref[0] = q.astype(jnp.bfloat16)
    gate = jnp.dot(xqn, wp_ref[:, 3 * CH :], preferred_element_type=jnp.float32)
    gate_ref[0] = jax.nn.sigmoid(gate + gb_ref[...])


def prepare(x, xq, gain, wp, gb):
    nrow, keys, _ = x.shape
    nq = xq.shape[1]
    outs = [
        jax.ShapeDtypeStruct((nrow, CH, keys), jnp.bfloat16),
        jax.ShapeDtypeStruct((nrow, keys, CH), jnp.bfloat16),
        jax.ShapeDtypeStruct((nrow, nq, CH), jnp.bfloat16),
        jax.ShapeDtypeStruct((nrow, nq, CH), jnp.float32),
    ]
    small = [gain[None], wp, gb[None]]
    return pl.pallas_call(
        prepare_kernel,
        grid=(nrow,),
        in_specs=[by_row(x), by_row(xq)] + [whole(a) for a in small],
        out_specs=[by_row(a) for a in outs],
        out_shape=outs,
        compiler_params=pltpu.CompilerParams(vmem_limit_bytes=16 << 20),
        cost_estimate=pl.CostEstimate(
            flops=4 * 10**9, bytes_accessed=6 << 20, transcendentals=nrow * nq * CH
        ),
        name="prepare",
    )(x, xq, *small)


def attention_kernel(nblk, ndone, stack, blk_ref, done_blk_ref, kt_ref, v_ref, q_ref, gate_ref, xq_ref, *refs):
    bias_refs = refs[:nblk]
    wo_ref, ob_ref = refs[nblk : nblk + 2]
    done_refs = refs[nblk + 2 : nblk + 2 + ndone]
    out_ref, biasf = refs[nblk + 2 + ndone :]
    half = bias_refs[0].shape[0]
    rows = bias_refs[0].shape[1] // 2
    block = rows // HEADS
    nq = nblk * block

    @pl.when(pl.program_id(0) == 0)
    def _():
        at = lax.broadcasted_iota(jnp.int32, (rows, 2 * rows), 0)
        to = lax.broadcasted_iota(jnp.int32, (rows, 2 * rows), 1)
        for s in range(2):
            pick = (to == at + s * rows).astype(jnp.bfloat16)
            for b in range(nblk):
                part = lax.dot_general(
                    pick, bias_refs[b][...], NT, preferred_element_type=jnp.float32
                )
                for h in range(HEADS):
                    biasf[
                        pl.ds(h * nq + b * block, block), pl.ds(s * half, half)
                    ] = part[h * block : (h + 1) * block] * LOG2E

    kt = kt_ref[0]
    v = v_ref[0]
    starts = [pl.multiple_of(blk_ref[b] * block, 16) for b in range(nblk)]
    q = jnp.concatenate([q_ref[0, pl.ds(t, block), :] for t in starts], axis=0)
    head_of = lax.broadcasted_iota(jnp.int32, q.shape, 1) // WIDTH
    mixed = jnp.zeros(q.shape, jnp.float32)
    for h0 in range(0, HEADS, stack):
        qh = jnp.concatenate(
            [jnp.where(head_of == h, q, jnp.zeros_like(q)) for h in range(h0, h0 + stack)], axis=0
        )
        s = jnp.dot(qh, kt, preferred_element_type=jnp.float32)
        s = s * (WIDTH**-0.5 * LOG2E) + biasf[h0 * nq : (h0 + stack) * nq]
        e = jnp.exp2(s - jnp.max(s, axis=-1, keepdims=True))
        p = (e * (1.0 / jnp.sum(e, axis=-1, keepdims=True))).astype(jnp.bfloat16)
        o = jnp.dot(p, v, preferred_element_type=jnp.float32)
        for t in range(stack):
            mixed = jnp.where(head_of == h0 + t, o[t * nq : (t + 1) * nq], mixed)
    gate = jnp.concatenate([gate_ref[0, pl.ds(t, block), :] for t in starts], axis=0)
    xq = jnp.concatenate([xq_ref[0, pl.ds(t, block), :] for t in starts], axis=0)
    gated = (mixed * gate).astype(jnp.bfloat16)
    y = jnp.dot(gated, wo_ref[...], preferred_element_type=jnp.float32) + ob_ref[...]
    y = (xq.astype(jnp.float32) + y).astype(jnp.bfloat16)
    if out_ref.shape[1] == nq:
        out_ref[0] = y
    else:
        for b in range(nblk):
            out_ref[0, pl.ds(starts[b], block), :] = y[b * block : (b + 1) * block]
        at = 0
        for ref in done_refs:
            for b in range(ref.shape[1] // block):
                t = pl.multiple_of(done_blk_ref[at] * block, 16)
                out_ref[0, pl.ds(t, block), :] = ref[0, b * block : (b + 1) * block, :]
                at += 1


def attend(ids, parts, xq, biases, wo, ob, done_ids, done, whole_out, stack):
    nrow, _, keys = parts[0].shape
    nblk = len(biases)
    nq = nblk * biases[0].shape[1] // 2 // HEADS
    out = jax.ShapeDtypeStruct((nrow, xq.shape[1] if whole_out else nq, CH), jnp.bfloat16)
    small = [wo, ob[None]]
    return pl.pallas_call(
        functools.partial(attention_kernel, nblk, len(done), stack),
        grid_spec=pltpu.PrefetchScalarGridSpec(
            num_scalar_prefetch=2,
            grid=(nrow,),
            in_specs=[by_row(a) for a in parts]
            + [by_row(xq)]
            + [whole(a) for a in list(biases) + small]
            + [by_row(a) for a in done],
            out_specs=by_row(out),
            scratch_shapes=[pltpu.VMEM((HEADS * nq, keys), jnp.float32)],
        ),
        out_shape=out,
        compiler_params=pltpu.CompilerParams(vmem_limit_bytes=40 << 20),
        cost_estimate=pl.CostEstimate(
            flops=nblk * 28 * 10**8, bytes_accessed=6 << 20, transcendentals=nrow * HEADS * nq * keys
        ),
        name="attend",
    )(ids, done_ids, *parts, xq, *biases, *small, *done)


def attention(ids, x, xq, biases, gain, wp, gb, wo, ob):
    parts = prepare(x, xq, gain, wp, gb)
    done, at = [], 0
    for n in CALLS:
        last = at + n == len(biases)
        y = attend(
            ids[at : at + n],
            parts,
            xq,
            biases[at : at + n],
            wo,
            ob,
            ids[: max(at, 1)],
            done if last else [],
            last,
            min(HEADS, max(1, 8 // n)),
        )
        done.append(y)
        at += n
    return done[-1]


def solution(mesh):
    nr, nc = mesh.shape["row"], mesh.shape["col"]
    ng = nc // 2
    same_core_col = [[2 * g + c for g in range(ng)] for c in range(2)]
    same_core_all = [[r * nc + 2 * g + c for r in range(nr) for g in range(ng)] for c in range(2)]
    swap_core = [(i, i ^ 1) for i in range(nc)]
    turns = ((0, 1), (0, 3), (1, 0), (0, 2), (1, 1), (1, 3), (1, 2))

    def turned(i, dx, dy):
        return ((i // 4) ^ dx) * 4 + (i % 4 + dy) % 4

    def spread(bias):
        me = lax.axis_index("row")
        got, ids = [bias], [me]
        for dx, dy in turns:
            got.append(lax.ppermute(bias, "row", [(i, turned(i, dx, dy)) for i in range(nr)]))
            ids.append(((me // 4) ^ dx) * 4 + (me % 4 - dy + 4) % 4)
        return got, jnp.stack(ids).astype(jnp.int32)

    def per_device(pair, norm_gain, w_proj, w_bias, gate_bias, w_out, out_bias):
        core = lax.axis_index("col") % 2
        nrow = pair.shape[0] // ng
        ncol = pair.shape[1]
        keys = nc * ncol
        half = keys // 2
        normed = normalize(pair, norm_gain[0])
        local = jnp.einsum("qmc,ch->mhq", normed, w_bias[0], preferred_element_type=jnp.float32)
        local = local.astype(jnp.bfloat16).reshape(ncol, HEADS, 2, 2, ncol).transpose(0, 3, 1, 2, 4)
        local = jnp.where(core == 0, local, local[:, ::-1]).reshape(-1, CH)
        brow = local.shape[0]
        message = jnp.concatenate(
            [
                pair.reshape(ng, nrow * ncol, CH),
                jnp.broadcast_to(local[None], (ng, brow, CH)),
                jnp.zeros((ng, -brow % 16, CH), jnp.bfloat16),
            ],
            axis=1,
        )
        got = lax.all_to_all(message, "col", 0, 0, tiled=True, axis_index_groups=same_core_col)
        x_own = got[:, : nrow * ncol]
        x_other = lax.ppermute(x_own, "col", swap_core)
        bias = got[:, nrow * ncol : nrow * ncol + brow].reshape(half, 2, half // 2)
        bias_other = lax.ppermute(bias[:, 1], "col", swap_core)
        bias = jnp.concatenate([bias[:, 0], bias_other], axis=1)
        biases, ids = spread(bias)
        x = jnp.stack([x_own, x_other]).reshape(2, ng, nrow, ncol, CH)
        x = x.transpose(2, 0, 1, 3, 4).reshape(nrow, keys, CH)
        first = attention(
            ids, x, x[:, :half], biases, norm_gain[0], w_proj[0], gate_bias[0], w_out[0], out_bias[0]
        )

        part = ncol // nr
        moved = first.reshape(nrow, ng, nr, part, CH).transpose(2, 1, 0, 3, 4)
        moved = moved.reshape(nr, ng, nrow * part, CH)
        normed = normalize(first, norm_gain[1])
        local = jnp.einsum("mqc,ch->mhq", normed, w_bias[1], preferred_element_type=jnp.float32)
        local = local.astype(jnp.bfloat16).reshape(nrow, HEADS, nr, half // nr).transpose(2, 0, 1, 3)
        local = local.reshape(nr, 1, -1, CH)
        brow = local.shape[2]
        message = jnp.concatenate(
            [
                moved,
                jnp.broadcast_to(local, (nr, ng, brow, CH)),
                jnp.zeros((nr, ng, -(brow + nrow * part) % 16, CH), jnp.bfloat16),
            ],
            axis=2,
        ).reshape(nr * ng, -1, CH)
        got = lax.all_to_all(
            message, ("row", "col"), 0, 0, tiled=True, axis_index_groups=same_core_all
        )
        x_own = got[:, : nrow * part].reshape(keys, part, CH).transpose(1, 0, 2)
        x_other = lax.ppermute(x_own, "col", swap_core)
        bias = got[:, nrow * part : nrow * part + brow].reshape(2, half, half // 2)
        bias = jnp.concatenate([bias[0], bias[1]], axis=1)
        biases, ids = spread(bias)
        x = jnp.concatenate([x_own, x_other])
        xq = x.reshape(2 * part, ng, 2, ncol, CH)
        xq = jnp.where(core == 0, xq[:, :, 0], xq[:, :, 1]).reshape(2 * part, half, CH)
        last = attention(
            ids, x, xq, biases, norm_gain[1], w_proj[1], gate_bias[1], w_out[1], out_bias[1]
        )

        own = last[:part]
        other = lax.ppermute(last[part:], "col", swap_core)
        both = jnp.stack([jnp.where(core == 0, own, other), jnp.where(core == 0, other, own)])
        both = both.reshape(2, part, nr, half // nr, CH).transpose(2, 0, 1, 3, 4)
        got = lax.all_to_all(both.reshape(nr, -1, CH), "row", 0, 0, tiled=True)
        got = got.reshape(nr, 2, part, 2, ncol, CH)
        return got.transpose(3, 1, 4, 0, 2, 5).reshape(pair.shape)

    return jax.shard_map(
        per_device,
        mesh=mesh,
        in_specs=(P("row", "col", None), P(), P(), P(), P(), P(), P()),
        out_specs=P("row", "col", None),
        check_vma=False,
    )
```

```python
import functools

import jax
import jax.numpy as jnp
from jax import lax
from jax.experimental import pallas as pl
from jax.experimental.pallas import tpu as pltpu
from jax.sharding import PartitionSpec as P

HEADS = 4
WIDTH = 32
CH = 128
LOG2E = 1.4426950408889634
CALLS = (3, 3, 2)
NT = (((1,), (1,)), ((), ()))


def normalize(values, gain):
    values = values.astype(jnp.float32)
    center = jnp.mean(values, axis=-1, keepdims=True)
    spread = jnp.mean((values - center) ** 2, axis=-1, keepdims=True)
    return ((values - center) * lax.rsqrt(spread + 1e-05) * gain).astype(jnp.bfloat16)


def whole(a):
    return pl.BlockSpec(a.shape, lambda i, *_: (0,) * a.ndim)


def by_row(a):
    return pl.BlockSpec((1,) + a.shape[1:], lambda i, *_: (i, 0, 0))


def by_block(a):
    return pl.BlockSpec((a.shape[0], 1) + a.shape[2:], lambda i, *_: (0, i, 0, 0))


def prepare_kernel(x_ref, xq_ref, gain_ref, wp_ref, gb_ref, kt_ref, v_ref, q_ref, gate_ref):
    gain = gain_ref[...]
    xn = normalize(x_ref[0], gain)
    k = jnp.dot(xn, wp_ref[:, CH : 2 * CH], preferred_element_type=jnp.float32)
    kt_ref[0] = k.astype(jnp.bfloat16).T
    v = jnp.dot(xn, wp_ref[:, 2 * CH : 3 * CH], preferred_element_type=jnp.float32)
    v_ref[0] = v.astype(jnp.bfloat16)
    xqn = normalize(xq_ref[0], gain)
    q = jnp.dot(xqn, wp_ref[:, :CH], preferred_element_type=jnp.float32)
    q_ref[0] = q.astype(jnp.bfloat16)
    gate = jnp.dot(xqn, wp_ref[:, 3 * CH :], preferred_element_type=jnp.float32)
    gate_ref[0] = jax.nn.sigmoid(gate + gb_ref[...])


def prepare(x, xq, gain, wp, gb):
    nrow, keys, _ = x.shape
    nq = xq.shape[1]
    outs = [
        jax.ShapeDtypeStruct((nrow, CH, keys), jnp.bfloat16),
        jax.ShapeDtypeStruct((nrow, keys, CH), jnp.bfloat16),
        jax.ShapeDtypeStruct((nrow, nq, CH), jnp.bfloat16),
        jax.ShapeDtypeStruct((nrow, nq, CH), jnp.float32),
    ]
    small = [gain[None], wp, gb[None]]
    return pl.pallas_call(
        prepare_kernel,
        grid=(nrow,),
        in_specs=[by_row(x), by_row(xq)] + [whole(a) for a in small],
        out_specs=[by_row(a) for a in outs],
        out_shape=outs,
        compiler_params=pltpu.CompilerParams(vmem_limit_bytes=16 << 20),
        cost_estimate=pl.CostEstimate(
            flops=4 * 10**9, bytes_accessed=6 << 20, transcendentals=nrow * nq * CH
        ),
        name="prepare",
    )(x, xq, *small)


def attention_kernel(nblk, ndone, stack, blk_ref, done_blk_ref, kt_ref, v_ref, q_ref, gate_ref, xq_ref, *refs):
    bias_refs = refs[:nblk]
    wo_ref, ob_ref = refs[nblk : nblk + 2]
    done_refs = refs[nblk + 2 : nblk + 2 + ndone]
    out_ref, biasf = refs[nblk + 2 + ndone :]
    half = bias_refs[0].shape[0]
    rows = bias_refs[0].shape[1] // 2
    block = rows // HEADS
    nq = nblk * block

    @pl.when(pl.program_id(0) == 0)
    def _():
        at = lax.broadcasted_iota(jnp.int32, (rows, 2 * rows), 0)
        to = lax.broadcasted_iota(jnp.int32, (rows, 2 * rows), 1)
        for s in range(2):
            pick = (to == at + s * rows).astype(jnp.bfloat16)
            for b in range(nblk):
                part = lax.dot_general(
                    pick, bias_refs[b][...], NT, preferred_element_type=jnp.float32
                )
                for h in range(HEADS):
                    biasf[
                        pl.ds(h * nq + b * block, block), pl.ds(s * half, half)
                    ] = part[h * block : (h + 1) * block] * LOG2E

    kt = kt_ref[0]
    v = v_ref[0]
    starts = [pl.multiple_of(blk_ref[b] * block, 16) for b in range(nblk)]
    q = jnp.concatenate([q_ref[0, pl.ds(t, block), :] for t in starts], axis=0)
    head_of = lax.broadcasted_iota(jnp.int32, q.shape, 1) // WIDTH
    mixed = jnp.zeros(q.shape, jnp.float32)
    for h0 in range(0, HEADS, stack):
        qh = jnp.concatenate(
            [jnp.where(head_of == h, q, jnp.zeros_like(q)) for h in range(h0, h0 + stack)], axis=0
        )
        s = jnp.dot(qh, kt, preferred_element_type=jnp.float32)
        s = s * (WIDTH**-0.5 * LOG2E) + biasf[h0 * nq : (h0 + stack) * nq]
        e = jnp.exp2(s - jnp.max(s, axis=-1, keepdims=True))
        p = (e * (1.0 / jnp.sum(e, axis=-1, keepdims=True))).astype(jnp.bfloat16)
        o = jnp.dot(p, v, preferred_element_type=jnp.float32)
        for t in range(stack):
            mixed = jnp.where(head_of == h0 + t, o[t * nq : (t + 1) * nq], mixed)
    gate = jnp.concatenate([gate_ref[0, pl.ds(t, block), :] for t in starts], axis=0)
    xq = jnp.concatenate([xq_ref[0, pl.ds(t, block), :] for t in starts], axis=0)
    gated = (mixed * gate).astype(jnp.bfloat16)
    y = jnp.dot(gated, wo_ref[...], preferred_element_type=jnp.float32) + ob_ref[...]
    y = (xq.astype(jnp.float32) + y).astype(jnp.bfloat16)
    if len(out_ref.shape) == 4:
        for b in range(nblk):
            out_ref[b, 0] = y[b * block : (b + 1) * block]
    else:
        for b in range(nblk):
            out_ref[0, pl.ds(starts[b], block), :] = y[b * block : (b + 1) * block]
        at = 0
        for ref in done_refs:
            for b in range(ref.shape[0]):
                t = pl.multiple_of(done_blk_ref[at] * block, 16)
                out_ref[0, pl.ds(t, block), :] = ref[b, 0]
                at += 1


def attend(ids, parts, xq, biases, wo, ob, done_ids, done, whole_out, stack):
    nrow, _, keys = parts[0].shape
    nblk = len(biases)
    nq = nblk * biases[0].shape[1] // 2 // HEADS
    shape = xq.shape if whole_out else (nblk, nrow, nq // nblk, CH)
    out = jax.ShapeDtypeStruct(shape, jnp.bfloat16)
    small = [wo, ob[None]]
    return pl.pallas_call(
        functools.partial(attention_kernel, nblk, len(done), stack),
        grid_spec=pltpu.PrefetchScalarGridSpec(
            num_scalar_prefetch=2,
            grid=(nrow,),
            in_specs=[by_row(a) for a in parts]
            + [by_row(xq)]
            + [whole(a) for a in list(biases) + small]
            + [by_block(a) for a in done],
            out_specs=by_row(out) if whole_out else by_block(out),
            scratch_shapes=[pltpu.VMEM((HEADS * nq, keys), jnp.float32)],
        ),
        out_shape=out,
        compiler_params=pltpu.CompilerParams(vmem_limit_bytes=40 << 20),
        cost_estimate=pl.CostEstimate(
            flops=nblk * 28 * 10**8, bytes_accessed=6 << 20, transcendentals=nrow * HEADS * nq * keys
        ),
        name="attend",
    )(ids, done_ids, *parts, xq, *biases, *small, *done)


def attention(ids, x, xq, biases, gain, wp, gb, wo, ob):
    parts = prepare(x, xq, gain, wp, gb)
    done, at = [], 0
    for n in CALLS:
        last = at + n == len(biases)
        y = attend(
            ids[at : at + n],
            parts,
            xq,
            biases[at : at + n],
            wo,
            ob,
            ids[: max(at, 1)],
            done if last else [],
            last,
            min(HEADS, max(1, 8 // n)),
        )
        done.append(y)
        at += n
    return done[-1]


def solution(mesh):
    nr, nc = mesh.shape["row"], mesh.shape["col"]
    ng = nc // 2
    same_core_col = [[2 * g + c for g in range(ng)] for c in range(2)]
    same_core_all = [[r * nc + 2 * g + c for r in range(nr) for g in range(ng)] for c in range(2)]
    swap_core = [(i, i ^ 1) for i in range(nc)]
    across = [
        (r * nc + c, (r ^ (nr // 2)) * nc + (c ^ (nc // 2))) for r in range(nr) for c in range(nc)
    ]
    ny = nr // 2

    def along_y(block, dy):
        return lax.ppermute(
            block, "row", [(i, i // ny * ny + (i + dy) % ny) for i in range(nr)]
        )

    def spread(bias):
        me = lax.axis_index("row")
        ids = lambda dx, dy: ((me // ny) ^ dx) * ny + (me + ny - dy) % ny
        over = lax.ppermute(bias, ("row", "col"), across)
        got = [bias, along_y(bias, 1), along_y(bias, 3), over, along_y(bias, 2)]
        got += [along_y(over, dy) for dy in (1, 3, 2)]
        order = [ids(0, 0), ids(0, 1), ids(0, 3), ids(1, 0), ids(0, 2)]
        order += [ids(1, dy) for dy in (1, 3, 2)]
        return got, jnp.stack(order).astype(jnp.int32)

    def per_device(pair, norm_gain, w_proj, w_bias, gate_bias, w_out, out_bias):
        core = lax.axis_index("col") % 2
        nrow = pair.shape[0] // ng
        ncol = pair.shape[1]
        keys = nc * ncol
        half = keys // 2
        normed = normalize(pair, norm_gain[0])
        local = jnp.einsum("qmc,ch->mhq", normed, w_bias[0], preferred_element_type=jnp.float32)
        local = local.astype(jnp.bfloat16).reshape(ncol, HEADS, 2, 2, ncol).transpose(0, 3, 1, 2, 4)
        local = jnp.where(core == 0, local, local[:, ::-1]).reshape(-1, CH)
        brow = local.shape[0]
        message = jnp.concatenate(
            [
                pair.reshape(ng, nrow * ncol, CH),
                jnp.broadcast_to(local[None], (ng, brow, CH)),
                jnp.zeros((ng, -brow % 16, CH), jnp.bfloat16),
            ],
            axis=1,
        )
        got = lax.all_to_all(message, "col", 0, 0, tiled=True, axis_index_groups=same_core_col)
        x_own = got[:, : nrow * ncol]
        x_other = lax.ppermute(x_own, "col", swap_core)
        bias = got[:, nrow * ncol : nrow * ncol + brow].reshape(half, 2, half // 2)
        bias_other = lax.ppermute(bias[:, 1], "col", swap_core)
        bias = jnp.concatenate([bias[:, 0], bias_other], axis=1)
        biases, ids = spread(bias)
        x = jnp.stack([x_own, x_other]).reshape(2, ng, nrow, ncol, CH)
        x = x.transpose(2, 0, 1, 3, 4).reshape(nrow, keys, CH)
        first = attention(
            ids, x, x[:, :half], biases, norm_gain[0], w_proj[0], gate_bias[0], w_out[0], out_bias[0]
        )

        part = ncol // nr
        moved = first.reshape(nrow, ng, nr, part, CH).transpose(2, 1, 0, 3, 4)
        moved = moved.reshape(nr, ng, nrow * part, CH)
        normed = normalize(first, norm_gain[1])
        local = jnp.einsum("mqc,ch->mhq", normed, w_bias[1], preferred_element_type=jnp.float32)
        local = local.astype(jnp.bfloat16).reshape(nrow, HEADS, nr, half // nr).transpose(2, 0, 1, 3)
        local = local.reshape(nr, 1, -1, CH)
        brow = local.shape[2]
        message = jnp.concatenate(
            [
                moved,
                jnp.broadcast_to(local, (nr, ng, brow, CH)),
                jnp.zeros((nr, ng, -(brow + nrow * part) % 16, CH), jnp.bfloat16),
            ],
            axis=2,
        ).reshape(nr * ng, -1, CH)
        got = lax.all_to_all(
            message, ("row", "col"), 0, 0, tiled=True, axis_index_groups=same_core_all
        )
        x_own = got[:, : nrow * part].reshape(keys, part, CH).transpose(1, 0, 2)
        x_other = lax.ppermute(x_own, "col", swap_core)
        bias = got[:, nrow * part : nrow * part + brow].reshape(2, half, half // 2)
        bias = jnp.concatenate([bias[0], bias[1]], axis=1)
        biases, ids = spread(bias)
        x = jnp.concatenate([x_own, x_other])
        xq = x.reshape(2 * part, ng, 2, ncol, CH)
        xq = jnp.where(core == 0, xq[:, :, 0], xq[:, :, 1]).reshape(2 * part, half, CH)
        last = attention(
            ids, x, xq, biases, norm_gain[1], w_proj[1], gate_bias[1], w_out[1], out_bias[1]
        )

        own = last[:part]
        other = lax.ppermute(last[part:], "col", swap_core)
        both = jnp.stack([jnp.where(core == 0, own, other), jnp.where(core == 0, other, own)])
        both = both.reshape(2, part, nr, half // nr, CH).transpose(2, 0, 1, 3, 4)
        got = lax.all_to_all(both.reshape(nr, -1, CH), "row", 0, 0, tiled=True)
        got = got.reshape(nr, 2, part, 2, ncol, CH)
        return got.transpose(3, 1, 4, 0, 2, 5).reshape(pair.shape)

    return jax.shard_map(
        per_device,
        mesh=mesh,
        in_specs=(P("row", "col", None), P(), P(), P(), P(), P(), P()),
        out_specs=P("row", "col", None),
        check_vma=False,
    )
```

```python
import functools

import jax
import jax.numpy as jnp
from jax import lax
from jax.experimental import pallas as pl
from jax.experimental.pallas import tpu as pltpu
from jax.sharding import PartitionSpec as P

HEADS = 4
WIDTH = 32
CH = 128
LOG2E = 1.4426950408889634
CALLS = (4, 2, 2)
NT = (((1,), (1,)), ((), ()))


def normalize(values, gain):
    values = values.astype(jnp.float32)
    center = jnp.mean(values, axis=-1, keepdims=True)
    spread = jnp.mean((values - center) ** 2, axis=-1, keepdims=True)
    return ((values - center) * lax.rsqrt(spread + 1e-05) * gain).astype(jnp.bfloat16)


def whole(a):
    return pl.BlockSpec(a.shape, lambda i, *_: (0,) * a.ndim)


def by_row(a):
    return pl.BlockSpec((1,) + a.shape[1:], lambda i, *_: (i, 0, 0))


def by_pair(a):
    return pl.BlockSpec((2,) + a.shape[1:], lambda i, *_: (i, 0, 0))


def by_block(a):
    return pl.BlockSpec((a.shape[0], 2) + a.shape[2:], lambda i, *_: (0, i, 0, 0))


def prepare_kernel(x_ref, xq_ref, gain_ref, wp_ref, gb_ref, kt_ref, v_ref, q_ref, gate_ref):
    gain = gain_ref[...]
    xn = normalize(x_ref[0], gain)
    k = jnp.dot(xn, wp_ref[:, CH : 2 * CH], preferred_element_type=jnp.float32)
    kt_ref[0] = k.astype(jnp.bfloat16).T
    v = jnp.dot(xn, wp_ref[:, 2 * CH : 3 * CH], preferred_element_type=jnp.float32)
    v_ref[0] = v.astype(jnp.bfloat16)
    xqn = normalize(xq_ref[0], gain)
    q = jnp.dot(xqn, wp_ref[:, :CH], preferred_element_type=jnp.float32)
    q_ref[0] = q.astype(jnp.bfloat16)
    gate = jnp.dot(xqn, wp_ref[:, 3 * CH :], preferred_element_type=jnp.float32)
    gate_ref[0] = jax.nn.sigmoid(gate + gb_ref[...])


def prepare(x, xq, gain, wp, gb):
    nrow, keys, _ = x.shape
    nq = xq.shape[1]
    outs = [
        jax.ShapeDtypeStruct((nrow, CH, keys), jnp.bfloat16),
        jax.ShapeDtypeStruct((nrow, keys, CH), jnp.bfloat16),
        jax.ShapeDtypeStruct((nrow, nq, CH), jnp.bfloat16),
        jax.ShapeDtypeStruct((nrow, nq, CH), jnp.float32),
    ]
    small = [gain[None], wp, gb[None]]
    return pl.pallas_call(
        prepare_kernel,
        grid=(nrow,),
        in_specs=[by_row(x), by_row(xq)] + [whole(a) for a in small],
        out_specs=[by_row(a) for a in outs],
        out_shape=outs,
        compiler_params=pltpu.CompilerParams(vmem_limit_bytes=16 << 20),
        cost_estimate=pl.CostEstimate(
            flops=4 * 10**9, bytes_accessed=6 << 20, transcendentals=nrow * nq * CH
        ),
        name="prepare",
    )(x, xq, *small)


def attention_kernel(nblk, ndone, stack, nnext, blk_ref, done_blk_ref, kt_ref, v_ref, q_ref, gate_ref, xq_ref, *refs):
    bias_refs = refs[:nblk]
    wo_ref, ob_ref = refs[nblk : nblk + 2]
    done_refs = refs[nblk + 2 : nblk + 2 + ndone]
    next_refs = refs[nblk + 2 + ndone : nblk + 2 + ndone + nnext]
    out_ref, *next_out, biasf = refs[nblk + 2 + ndone + nnext :]
    half = bias_refs[0].shape[0]
    rows = bias_refs[0].shape[1] // 2
    block = rows // HEADS
    nq = nblk * block

    @pl.when(pl.program_id(0) == 0)
    def _():
        for b in range(nblk):
            part = bias_refs[b][...].astype(jnp.float32).T * LOG2E
            for s in range(2):
                for h in range(HEADS):
                    at = s * rows + h * block
                    biasf[pl.ds(h * nq + b * block, block), pl.ds(s * half, half)] = part[
                        at : at + block
                    ]

    pair = range(2)
    kt = jnp.concatenate([kt_ref[u] for u in pair], axis=0)
    v = jnp.concatenate([v_ref[u] for u in pair], axis=1)
    starts = [pl.multiple_of(blk_ref[b] * block, 16) for b in range(nblk)]

    def picked(ref, u):
        return jnp.concatenate([ref[u, pl.ds(t, block), :] for t in starts], axis=0)

    q = [picked(q_ref, u) for u in pair]
    head_of = lax.broadcasted_iota(jnp.int32, q[0].shape, 1) // WIDTH
    zero = jnp.zeros_like(q[0])
    mixed = [jnp.zeros(q[0].shape, jnp.float32) for _ in pair]
    for h0 in range(0, HEADS, stack):
        heads = range(h0, h0 + stack)
        here = [jnp.where(head_of == h, q[0], zero) for h in heads]
        there = [jnp.where(head_of == h, q[1], zero) for h in heads]
        qh = jnp.concatenate(
            [jnp.concatenate([t, zero], axis=1) for t in here]
            + [jnp.concatenate([zero, t], axis=1) for t in there],
            axis=0,
        )
        s = jnp.dot(qh, kt, preferred_element_type=jnp.float32)
        bias = biasf[h0 * nq : (h0 + stack) * nq]
        s = s * (WIDTH**-0.5 * LOG2E) + jnp.concatenate([bias, bias], axis=0)
        e = jnp.exp2(s - jnp.max(s, axis=-1, keepdims=True))
        p = (e * (1.0 / jnp.sum(e, axis=-1, keepdims=True))).astype(jnp.bfloat16)
        o = jnp.dot(p, v, preferred_element_type=jnp.float32)
        for u in pair:
            for n, h in enumerate(heads):
                at = (u * stack + n) * nq
                part = o[at : at + nq, u * CH : (u + 1) * CH]
                mixed[u] = jnp.where(head_of == h, part, mixed[u])
    for u in pair:
        gated = (mixed[u] * picked(gate_ref, u)).astype(jnp.bfloat16)
        y = jnp.dot(gated, wo_ref[...], preferred_element_type=jnp.float32) + ob_ref[...]
        y = (picked(xq_ref, u).astype(jnp.float32) + y).astype(jnp.bfloat16)
        for b in range(nblk):
            part = y[b * block : (b + 1) * block]
            if len(out_ref.shape) == 4:
                out_ref[b, u] = part
            else:
                out_ref[u, pl.ds(starts[b], block), :] = part
        at = 0
        for ref in done_refs:
            for b in range(ref.shape[0]):
                t = pl.multiple_of(done_blk_ref[at] * block, 16)
                out_ref[u, pl.ds(t, block), :] = ref[b, u]
                at += 1
        if nnext:
            normed = normalize(out_ref[u], next_refs[0][...])
            next_out[0][u] = lax.dot_general(
                next_refs[1][...], normed, NT, preferred_element_type=jnp.float32
            ).astype(jnp.bfloat16)


def attend(ids, parts, xq, biases, wo, ob, done_ids, done, whole_out, stack, following):
    nrow, _, keys = parts[0].shape
    nblk = len(biases)
    nq = nblk * biases[0].shape[1] // 2 // HEADS
    shape = xq.shape if whole_out else (nblk, nrow, nq // nblk, CH)
    out = [jax.ShapeDtypeStruct(shape, jnp.bfloat16)]
    out_specs = [by_pair(out[0]) if whole_out else by_block(out[0])]
    if following:
        out.append(jax.ShapeDtypeStruct((nrow, 8, xq.shape[1]), jnp.bfloat16))
        out_specs.append(by_pair(out[1]))
    small = [wo, ob[None]]
    return pl.pallas_call(
        functools.partial(attention_kernel, nblk, len(done), stack, len(following)),
        grid_spec=pltpu.PrefetchScalarGridSpec(
            num_scalar_prefetch=2,
            grid=(nrow // 2,),
            in_specs=[by_pair(a) for a in parts]
            + [by_pair(xq)]
            + [whole(a) for a in list(biases) + small]
            + [by_block(a) for a in done]
            + [whole(a) for a in following],
            out_specs=out_specs,
            scratch_shapes=[pltpu.VMEM((HEADS * nq, keys), jnp.float32)],
        ),
        out_shape=out,
        compiler_params=pltpu.CompilerParams(vmem_limit_bytes=40 << 20),
        cost_estimate=pl.CostEstimate(
            flops=nblk * 28 * 10**8, bytes_accessed=6 << 20, transcendentals=nrow * HEADS * nq * keys
        ),
        name="attend",
    )(ids, done_ids, *parts, xq, *biases, *small, *done, *following)


def attention(ids, x, xq, biases, gain, wp, gb, wo, ob, following):
    parts = prepare(x, xq, gain, wp, gb)
    done, at = [], 0
    for n in CALLS:
        last = at + n == len(biases)
        out = attend(
            ids[at : at + n],
            parts,
            xq,
            biases[at : at + n],
            wo,
            ob,
            ids[: max(at, 1)],
            done if last else [],
            last,
            1 if n > 2 else 2,
            following if last else [],
        )
        done.append(out[0])
        at += n
    return out


def solution(mesh):
    nr, nc = mesh.shape["row"], mesh.shape["col"]
    ng = nc // 2
    same_core_col = [[2 * g + c for g in range(ng)] for c in range(2)]
    same_core_all = [[r * nc + 2 * g + c for r in range(nr) for g in range(ng)] for c in range(2)]
    swap_core = [(i, i ^ 1) for i in range(nc)]
    ny = nr // 2
    across = [(r * nc + c, (r + ny) % nr * nc + (c ^ ng)) for r in range(nr) for c in range(nc)]

    def along_y(block, dy):
        return lax.ppermute(
            block, "row", [(i, i // ny * ny + (i + dy) % ny) for i in range(nr)]
        )

    def to_neighbour(block):
        return lax.ppermute(block, ("row", "col"), across)

    def spread(bias):
        near, far, over, two = along_y(bias, 1), along_y(bias, 3), to_neighbour(bias), along_y(bias, 2)
        got = [bias, near, far, over, two, along_y(over, 1), along_y(over, 3), to_neighbour(two)]
        x, y = lax.axis_index("row") // ny, lax.axis_index("row") % ny
        turns = ((0, 0), (0, 1), (0, 3), (1, 0), (0, 2), (1, 1), (1, 3), (1, 2))
        ids = [(x ^ dx) * ny + (y + ny - dy) % ny for dx, dy in turns]
        return got, jnp.stack(ids).astype(jnp.int32)

    def per_device(pair, norm_gain, w_proj, w_bias, gate_bias, w_out, out_bias):
        core = lax.axis_index("col") % 2
        nrow = pair.shape[0] // ng
        ncol = pair.shape[1]
        keys = nc * ncol
        half = keys // 2
        normed = normalize(pair, norm_gain[0])
        local = jnp.einsum("qmc,ch->mhq", normed, w_bias[0], preferred_element_type=jnp.float32)
        local = local.astype(jnp.bfloat16).reshape(ncol, HEADS, 2, 2, ncol).transpose(0, 3, 1, 2, 4)
        local = jnp.where(core == 0, local, local[:, ::-1]).reshape(-1, CH)
        brow = local.shape[0]
        message = jnp.concatenate(
            [
                pair.reshape(ng, nrow * ncol, CH),
                jnp.broadcast_to(local[None], (ng, brow, CH)),
                jnp.zeros((ng, -brow % 16, CH), jnp.bfloat16),
            ],
            axis=1,
        )
        got = lax.all_to_all(message, "col", 0, 0, tiled=True, axis_index_groups=same_core_col)
        x_own = got[:, : nrow * ncol]
        x_other = lax.ppermute(x_own, "col", swap_core)
        bias = got[:, nrow * ncol : nrow * ncol + brow].reshape(half, 2, half // 2)
        bias_other = lax.ppermute(bias[:, 1], "col", swap_core)
        bias = jnp.concatenate([bias[:, 0], bias_other], axis=1)
        biases, ids = spread(bias)
        x = jnp.stack([x_own, x_other]).reshape(2, ng, nrow, ncol, CH)
        x = x.transpose(2, 0, 1, 3, 4).reshape(nrow, keys, CH)
        following = [norm_gain[1][None], jnp.pad(w_bias[1].T, ((0, 8 - HEADS), (0, 0)))]
        args = (norm_gain[0], w_proj[0], gate_bias[0], w_out[0], out_bias[0], following)
        first, local = attention(ids, x, x[:, :half], biases, *args)

        part = ncol // nr
        moved = first.reshape(nrow, ng, nr, part, CH).transpose(2, 1, 0, 3, 4)
        moved = moved.reshape(nr, ng, nrow * part, CH)
        local = local[:, :HEADS].reshape(nrow, HEADS, nr, half // nr).transpose(2, 0, 1, 3)
        local = local.reshape(nr, 1, -1, CH)
        brow = local.shape[2]
        message = jnp.concatenate(
            [
                moved,
                jnp.broadcast_to(local, (nr, ng, brow, CH)),
                jnp.zeros((nr, ng, -(brow + nrow * part) % 16, CH), jnp.bfloat16),
            ],
            axis=2,
        ).reshape(nr * ng, -1, CH)
        got = lax.all_to_all(
            message, ("row", "col"), 0, 0, tiled=True, axis_index_groups=same_core_all
        )
        x_own = got[:, : nrow * part].reshape(keys, part, CH).transpose(1, 0, 2)
        x_other = lax.ppermute(x_own, "col", swap_core)
        bias = got[:, nrow * part : nrow * part + brow].reshape(2, half, half // 2)
        bias = jnp.concatenate([bias[0], bias[1]], axis=1)
        biases, ids = spread(bias)
        x = jnp.concatenate([x_own, x_other])
        xq = x.reshape(2 * part, ng, 2, ncol, CH)
        xq = jnp.where(core == 0, xq[:, :, 0], xq[:, :, 1]).reshape(2 * part, half, CH)
        args = (norm_gain[1], w_proj[1], gate_bias[1], w_out[1], out_bias[1], [])
        (last,) = attention(ids, x, xq, biases, *args)

        own = last[:part]
        other = lax.ppermute(last[part:], "col", swap_core)
        both = jnp.stack([jnp.where(core == 0, own, other), jnp.where(core == 0, other, own)])
        both = both.reshape(2, part, nr, half // nr, CH).transpose(2, 0, 1, 3, 4)
        got = lax.all_to_all(both.reshape(nr, -1, CH), "row", 0, 0, tiled=True)
        got = got.reshape(nr, 2, part, 2, ncol, CH)
        return got.transpose(3, 1, 4, 0, 2, 5).reshape(pair.shape)

    return jax.shard_map(
        per_device,
        mesh=mesh,
        in_specs=(P("row", "col", None), P(), P(), P(), P(), P(), P()),
        out_specs=P("row", "col", None),
        check_vma=False,
    )
```

```python
import functools

import jax
import jax.numpy as jnp
from jax import lax
from jax.experimental import pallas as pl
from jax.experimental.pallas import tpu as pltpu
from jax.sharding import PartitionSpec as P

HEADS = 4
WIDTH = 32
CH = 128
LOG2E = 1.4426950408889634
CALLS = (4, 4)
NT = (((1,), (1,)), ((), ()))


def normalize(values, gain):
    values = values.astype(jnp.float32)
    center = jnp.mean(values, axis=-1, keepdims=True)
    spread = jnp.mean((values - center) ** 2, axis=-1, keepdims=True)
    return ((values - center) * lax.rsqrt(spread + 1e-05) * gain).astype(jnp.bfloat16)


def whole(a):
    return pl.BlockSpec(a.shape, lambda i, *_: (0,) * a.ndim)


def by_row(a):
    return pl.BlockSpec((1,) + a.shape[1:], lambda i, *_: (i, 0, 0))


def by_pair(a):
    return pl.BlockSpec((2,) + a.shape[1:], lambda i, *_: (i, 0, 0))


def by_block(a):
    return pl.BlockSpec((a.shape[0], 2) + a.shape[2:], lambda i, *_: (0, i, 0, 0))


def prepare_kernel(x_ref, xq_ref, gain_ref, wp_ref, gb_ref, kt_ref, v_ref, q_ref, gate_ref):
    gain = gain_ref[...]
    xn = normalize(x_ref[0], gain)
    k = jnp.dot(xn, wp_ref[:, CH : 2 * CH], preferred_element_type=jnp.float32)
    kt_ref[0] = k.astype(jnp.bfloat16).T
    v = jnp.dot(xn, wp_ref[:, 2 * CH : 3 * CH], preferred_element_type=jnp.float32)
    v_ref[0] = v.astype(jnp.bfloat16)
    xqn = normalize(xq_ref[0], gain)
    q = jnp.dot(xqn, wp_ref[:, :CH], preferred_element_type=jnp.float32)
    q_ref[0] = q.astype(jnp.bfloat16)
    gate = jnp.dot(xqn, wp_ref[:, 3 * CH :], preferred_element_type=jnp.float32)
    gate_ref[0] = jax.nn.sigmoid(gate + gb_ref[...])


def prepare(x, xq, gain, wp, gb):
    nrow, keys, _ = x.shape
    nq = xq.shape[1]
    outs = [
        jax.ShapeDtypeStruct((nrow, CH, keys), jnp.bfloat16),
        jax.ShapeDtypeStruct((nrow, keys, CH), jnp.bfloat16),
        jax.ShapeDtypeStruct((nrow, nq, CH), jnp.bfloat16),
        jax.ShapeDtypeStruct((nrow, nq, CH), jnp.float32),
    ]
    small = [gain[None], wp, gb[None]]
    return pl.pallas_call(
        prepare_kernel,
        grid=(nrow,),
        in_specs=[by_row(x), by_row(xq)] + [whole(a) for a in small],
        out_specs=[by_row(a) for a in outs],
        out_shape=outs,
        compiler_params=pltpu.CompilerParams(vmem_limit_bytes=16 << 20),
        cost_estimate=pl.CostEstimate(
            flops=4 * 10**9, bytes_accessed=6 << 20, transcendentals=nrow * nq * CH
        ),
        name="prepare",
    )(x, xq, *small)


def attention_kernel(nblk, ndone, stack, nnext, blk_ref, done_blk_ref, kt_ref, v_ref, q_ref, gate_ref, xq_ref, *refs):
    bias_refs = refs[:nblk]
    wo_ref, ob_ref = refs[nblk : nblk + 2]
    done_refs = refs[nblk + 2 : nblk + 2 + ndone]
    next_refs = refs[nblk + 2 + ndone : nblk + 2 + ndone + nnext]
    out_ref, *next_out, biasf = refs[nblk + 2 + ndone + nnext :]
    half = bias_refs[0].shape[0]
    rows = bias_refs[0].shape[1] // 2
    block = rows // HEADS
    nq = nblk * block

    @pl.when(pl.program_id(0) == 0)
    def _():
        for b in range(nblk):
            part = bias_refs[b][...].astype(jnp.float32).T * LOG2E
            for s in range(2):
                for h in range(HEADS):
                    at = s * rows + h * block
                    biasf[pl.ds(h * nq + b * block, block), pl.ds(s * half, half)] = part[
                        at : at + block
                    ]

    pair = range(2)
    kt = jnp.concatenate([kt_ref[u] for u in pair], axis=0)
    v = jnp.concatenate([v_ref[u] for u in pair], axis=1)
    starts = [pl.multiple_of(blk_ref[b] * block, 16) for b in range(nblk)]

    def picked(ref, u):
        return jnp.concatenate([ref[u, pl.ds(t, block), :] for t in starts], axis=0)

    q = [picked(q_ref, u) for u in pair]
    head_of = lax.broadcasted_iota(jnp.int32, q[0].shape, 1) // WIDTH
    zero = jnp.zeros_like(q[0])
    mixed = [jnp.zeros(q[0].shape, jnp.float32) for _ in pair]
    for h0 in range(0, HEADS, stack):
        heads = range(h0, h0 + stack)
        here = [jnp.where(head_of == h, q[0], zero) for h in heads]
        there = [jnp.where(head_of == h, q[1], zero) for h in heads]
        qh = jnp.concatenate(
            [jnp.concatenate([t, zero], axis=1) for t in here]
            + [jnp.concatenate([zero, t], axis=1) for t in there],
            axis=0,
        )
        s = jnp.dot(qh, kt, preferred_element_type=jnp.float32)
        bias = biasf[h0 * nq : (h0 + stack) * nq]
        s = s * (WIDTH**-0.5 * LOG2E) + jnp.concatenate([bias, bias], axis=0)
        e = jnp.exp2(s - jnp.max(s, axis=-1, keepdims=True))
        p = (e * (1.0 / jnp.sum(e, axis=-1, keepdims=True))).astype(jnp.bfloat16)
        o = jnp.dot(p, v, preferred_element_type=jnp.float32)
        for u in pair:
            for n, h in enumerate(heads):
                at = (u * stack + n) * nq
                part = o[at : at + nq, u * CH : (u + 1) * CH]
                mixed[u] = jnp.where(head_of == h, part, mixed[u])
    for u in pair:
        gated = (mixed[u] * picked(gate_ref, u)).astype(jnp.bfloat16)
        y = jnp.dot(gated, wo_ref[...], preferred_element_type=jnp.float32) + ob_ref[...]
        y = (picked(xq_ref, u).astype(jnp.float32) + y).astype(jnp.bfloat16)
        for b in range(nblk):
            part = y[b * block : (b + 1) * block]
            if len(out_ref.shape) == 4:
                out_ref[b, u] = part
            else:
                out_ref[u, pl.ds(starts[b], block), :] = part
        at = 0
        for ref in done_refs:
            for b in range(ref.shape[0]):
                t = pl.multiple_of(done_blk_ref[at] * block, 16)
                out_ref[u, pl.ds(t, block), :] = ref[b, u]
                at += 1
        if nnext:
            normed = normalize(out_ref[u], next_refs[0][...])
            next_out[0][u] = lax.dot_general(
                next_refs[1][...], normed, NT, preferred_element_type=jnp.float32
            ).astype(jnp.bfloat16)


def attend(ids, parts, xq, biases, wo, ob, done_ids, done, whole_out, stack, following):
    nrow, _, keys = parts[0].shape
    nblk = len(biases)
    nq = nblk * biases[0].shape[1] // 2 // HEADS
    shape = xq.shape if whole_out else (nblk, nrow, nq // nblk, CH)
    out = [jax.ShapeDtypeStruct(shape, jnp.bfloat16)]
    out_specs = [by_pair(out[0]) if whole_out else by_block(out[0])]
    if following:
        out.append(jax.ShapeDtypeStruct((nrow, 8, xq.shape[1]), jnp.bfloat16))
        out_specs.append(by_pair(out[1]))
    small = [wo, ob[None]]
    return pl.pallas_call(
        functools.partial(attention_kernel, nblk, len(done), stack, len(following)),
        grid_spec=pltpu.PrefetchScalarGridSpec(
            num_scalar_prefetch=2,
            grid=(nrow // 2,),
            in_specs=[by_pair(a) for a in parts]
            + [by_pair(xq)]
            + [whole(a) for a in list(biases) + small]
            + [by_block(a) for a in done]
            + [whole(a) for a in following],
            out_specs=out_specs,
            scratch_shapes=[pltpu.VMEM((HEADS * nq, keys), jnp.float32)],
        ),
        out_shape=out,
        compiler_params=pltpu.CompilerParams(vmem_limit_bytes=40 << 20),
        cost_estimate=pl.CostEstimate(
            flops=nblk * 28 * 10**8, bytes_accessed=6 << 20, transcendentals=nrow * HEADS * nq * keys
        ),
        name="attend",
    )(ids, done_ids, *parts, xq, *biases, *small, *done, *following)


def attention(ids, parts, xq, biases, wo, ob, following):
    done, at = [], 0
    for n in CALLS:
        last = at + n == len(biases)
        out = attend(
            ids[at : at + n],
            parts,
            xq,
            biases[at : at + n],
            wo,
            ob,
            ids[: max(at, 1)],
            done if last else [],
            last,
            1 if n > 2 else 2,
            following if last else [],
        )
        done.append(out[0])
        at += n
    return out


def solution(mesh):
    nr, nc = mesh.shape["row"], mesh.shape["col"]
    ng = nc // 2
    same_core_col = [[2 * g + c for g in range(ng)] for c in range(2)]
    same_core_all = [[r * nc + 2 * g + c for r in range(nr) for g in range(ng)] for c in range(2)]
    swap_core = [(i, i ^ 1) for i in range(nc)]
    ny = nr // 2
    across = [(r * nc + c, (r + ny) % nr * nc + (c ^ ng)) for r in range(nr) for c in range(nc)]

    def along_y(block, dy):
        return lax.ppermute(
            block, "row", [(i, i // ny * ny + (i + dy) % ny) for i in range(nr)]
        )

    def to_neighbour(block):
        return lax.ppermute(block, ("row", "col"), across)

    def spread(bias):
        return [along_y(bias, 1), along_y(bias, 3), to_neighbour(bias), along_y(bias, 2)]

    def spread_on(bias, first, parts):
        near, far, over, two = first
        over, two, parts = lax.optimization_barrier((over, two, parts))
        got = [bias, near, far, over, two, along_y(over, 1), along_y(over, 3), to_neighbour(two)]
        x, y = lax.axis_index("row") // ny, lax.axis_index("row") % ny
        turns = ((0, 0), (0, 1), (0, 3), (1, 0), (0, 2), (1, 1), (1, 3), (1, 2))
        ids = [(x ^ dx) * ny + (y + ny - dy) % ny for dx, dy in turns]
        return got, jnp.stack(ids).astype(jnp.int32), parts

    def all_to_all_16(message):
        return lax.all_to_all(
            message, "col", 0, 0, tiled=True, axis_index_groups=same_core_col
        )

    def per_device(pair, norm_gain, w_proj, w_bias, gate_bias, w_out, out_bias):
        core = lax.axis_index("col") % 2
        nrow = pair.shape[0] // ng
        ncol = pair.shape[1]
        keys = nc * ncol
        half = keys // 2
        normed = normalize(pair, norm_gain[0])
        local = jnp.einsum("qmc,ch->mhq", normed, w_bias[0], preferred_element_type=jnp.float32)
        local = local.astype(jnp.bfloat16).reshape(ncol, HEADS, 2, 2, ncol).transpose(0, 3, 1, 2, 4)
        local = local.reshape(ncol, 2, -1)
        own = jnp.where(core == 0, local[:, 0], local[:, 1])
        other = jnp.where(core == 0, local[:, 1], local[:, 0])
        other = lax.ppermute(other, "col", swap_core)
        local = jnp.concatenate([own, other], axis=1).reshape(-1, CH)
        brow = local.shape[0]
        message = jnp.broadcast_to(local[None], (ng,) + local.shape)
        message = jnp.concatenate([pair.reshape(ng, nrow * ncol, CH), message], axis=1)
        got = all_to_all_16(message)
        x_own = got[:, : nrow * ncol]
        x_other = lax.ppermute(x_own, "col", swap_core)
        bias = got[:, nrow * ncol :].reshape(half, half)
        first_biases = spread(bias)
        x = jnp.stack([x_own, x_other]).reshape(2, ng, nrow, ncol, CH)
        x = x.transpose(2, 0, 1, 3, 4).reshape(nrow, keys, CH)
        following = [norm_gain[1][None], jnp.pad(w_bias[1].T, ((0, 8 - HEADS), (0, 0)))]
        xq = x[:, :half]
        parts = prepare(x, xq, norm_gain[0], w_proj[0], gate_bias[0])
        biases, ids, parts = spread_on(bias, first_biases, parts)
        first, local = attention(ids, parts, xq, biases, w_out[0], out_bias[0], following)

        part = ncol // nr
        moved = first.reshape(nrow, ng, nr, part, CH).transpose(2, 1, 0, 3, 4)
        moved = moved.reshape(nr, ng, nrow * part, CH)
        local = local[:, :HEADS].reshape(nrow, HEADS, nr, half // nr).transpose(2, 0, 1, 3)
        local = local.reshape(nr, 1, -1, CH)
        brow = local.shape[2]
        message = jnp.concatenate(
            [
                moved,
                jnp.broadcast_to(local, (nr, ng, brow, CH)),
                jnp.zeros((nr, ng, -(brow + nrow * part) % 16, CH), jnp.bfloat16),
            ],
            axis=2,
        ).reshape(nr * ng, -1, CH)
        got = lax.all_to_all(
            message, ("row", "col"), 0, 0, tiled=True, axis_index_groups=same_core_all
        )
        x_own = got[:, : nrow * part].reshape(keys, part, CH).transpose(1, 0, 2)
        x_other = lax.ppermute(x_own, "col", swap_core)
        bias = got[:, nrow * part : nrow * part + brow].reshape(2, half, half // 2)
        bias = jnp.concatenate([bias[0], bias[1]], axis=1)
        first_biases = spread(bias)
        x = jnp.concatenate([x_own, x_other])
        xq = x.reshape(2 * part, ng, 2, ncol, CH)
        xq = jnp.where(core == 0, xq[:, :, 0], xq[:, :, 1]).reshape(2 * part, half, CH)
        parts = prepare(x, xq, norm_gain[1], w_proj[1], gate_bias[1])
        biases, ids, parts = spread_on(bias, first_biases, parts)
        (last,) = attention(ids, parts, xq, biases, w_out[1], out_bias[1], [])

        own = last[:part]
        other = lax.ppermute(last[part:], "col", swap_core)
        both = jnp.stack([jnp.where(core == 0, own, other), jnp.where(core == 0, other, own)])
        both = both.reshape(2, part, nr, half // nr, CH).transpose(2, 0, 1, 3, 4)
        got = lax.all_to_all(both.reshape(nr, -1, CH), "row", 0, 0, tiled=True)
        got = got.reshape(nr, 2, part, 2, ncol, CH)
        return got.transpose(3, 1, 4, 0, 2, 5).reshape(pair.shape)

    return jax.shard_map(
        per_device,
        mesh=mesh,
        in_specs=(P("row", "col", None), P(), P(), P(), P(), P(), P()),
        out_specs=P("row", "col", None),
        check_vma=False,
    )
```

```python
import functools

import jax
import jax.numpy as jnp
from jax import lax
from jax.experimental import pallas as pl
from jax.experimental.pallas import tpu as pltpu
from jax.sharding import PartitionSpec as P

HEADS = 4
WIDTH = 32
CH = 128
LOG2E = 1.4426950408889634
CALLS = (3, 5)
NT = (((1,), (1,)), ((), ()))


def normalize(values, gain):
    values = values.astype(jnp.float32)
    center = jnp.mean(values, axis=-1, keepdims=True)
    spread = jnp.mean((values - center) ** 2, axis=-1, keepdims=True)
    return ((values - center) * lax.rsqrt(spread + 1e-05) * gain).astype(jnp.bfloat16)


def whole(a):
    return pl.BlockSpec(a.shape, lambda i, *_: (0,) * a.ndim)


def by_row(a):
    return pl.BlockSpec((1,) + a.shape[1:], lambda i, *_: (i, 0, 0))


def by_pair(a):
    return pl.BlockSpec((2,) + a.shape[1:], lambda i, *_: (i, 0, 0))


def by_block(a):
    return pl.BlockSpec((a.shape[0], 2) + a.shape[2:], lambda i, *_: (0, i, 0, 0))


def prepare_kernel(x_ref, xq_ref, gain_ref, wp_ref, gb_ref, kt_ref, v_ref, q_ref, gate_ref):
    gain = gain_ref[...]
    xn = normalize(x_ref[0], gain)
    k = jnp.dot(xn, wp_ref[:, CH : 2 * CH], preferred_element_type=jnp.float32)
    kt_ref[0] = k.astype(jnp.bfloat16).T
    v = jnp.dot(xn, wp_ref[:, 2 * CH : 3 * CH], preferred_element_type=jnp.float32)
    v_ref[0] = v.astype(jnp.bfloat16)
    xqn = normalize(xq_ref[0], gain)
    q = jnp.dot(xqn, wp_ref[:, :CH], preferred_element_type=jnp.float32)
    q_ref[0] = q.astype(jnp.bfloat16)
    gate = jnp.dot(xqn, wp_ref[:, 3 * CH :], preferred_element_type=jnp.float32)
    gate_ref[0] = jax.nn.sigmoid(gate + gb_ref[...])


def prepare(x, xq, gain, wp, gb):
    nrow, keys, _ = x.shape
    nq = xq.shape[1]
    outs = [
        jax.ShapeDtypeStruct((nrow, CH, keys), jnp.bfloat16),
        jax.ShapeDtypeStruct((nrow, keys, CH), jnp.bfloat16),
        jax.ShapeDtypeStruct((nrow, nq, CH), jnp.bfloat16),
        jax.ShapeDtypeStruct((nrow, nq, CH), jnp.float32),
    ]
    small = [gain[None], wp, gb[None]]
    return pl.pallas_call(
        prepare_kernel,
        grid=(nrow,),
        in_specs=[by_row(x), by_row(xq)] + [whole(a) for a in small],
        out_specs=[by_row(a) for a in outs],
        out_shape=outs,
        compiler_params=pltpu.CompilerParams(vmem_limit_bytes=16 << 20),
        cost_estimate=pl.CostEstimate(
            flops=4 * 10**9, bytes_accessed=6 << 20, transcendentals=nrow * nq * CH
        ),
        name="prepare",
    )(x, xq, *small)


def attention_kernel(nblk, ndone, stack, nnext, blk_ref, done_blk_ref, kt_ref, v_ref, q_ref, gate_ref, xq_ref, *refs):
    bias_refs = refs[:nblk]
    wo_ref, ob_ref = refs[nblk : nblk + 2]
    done_refs = refs[nblk + 2 : nblk + 2 + ndone]
    next_refs = refs[nblk + 2 + ndone : nblk + 2 + ndone + nnext]
    out_ref, *next_out, biasf = refs[nblk + 2 + ndone + nnext :]
    half = bias_refs[0].shape[0]
    rows = bias_refs[0].shape[1] // 2
    block = rows // HEADS
    nq = nblk * block

    @pl.when(pl.program_id(0) == 0)
    def _():
        for b in range(nblk):
            part = bias_refs[b][...].astype(jnp.float32).T * LOG2E
            for s in range(2):
                for h in range(HEADS):
                    at = s * rows + h * block
                    biasf[pl.ds(h * nq + b * block, block), pl.ds(s * half, half)] = part[
                        at : at + block
                    ]

    pair = range(2)
    kt = jnp.concatenate([kt_ref[u] for u in pair], axis=0)
    v = jnp.concatenate([v_ref[u] for u in pair], axis=1)
    starts = [pl.multiple_of(blk_ref[b] * block, 16) for b in range(nblk)]

    def picked(ref, u):
        return jnp.concatenate([ref[u, pl.ds(t, block), :] for t in starts], axis=0)

    q = [picked(q_ref, u) for u in pair]
    head_of = lax.broadcasted_iota(jnp.int32, q[0].shape, 1) // WIDTH
    zero = jnp.zeros_like(q[0])
    mixed = [jnp.zeros(q[0].shape, jnp.float32) for _ in pair]
    for h0 in range(0, HEADS, stack):
        heads = range(h0, h0 + stack)
        here = [jnp.where(head_of == h, q[0], zero) for h in heads]
        there = [jnp.where(head_of == h, q[1], zero) for h in heads]
        qh = jnp.concatenate(
            [jnp.concatenate([t, zero], axis=1) for t in here]
            + [jnp.concatenate([zero, t], axis=1) for t in there],
            axis=0,
        )
        s = jnp.dot(qh, kt, preferred_element_type=jnp.float32)
        bias = biasf[h0 * nq : (h0 + stack) * nq]
        s = s * (WIDTH**-0.5 * LOG2E) + jnp.concatenate([bias, bias], axis=0)
        e = jnp.exp2(s - jnp.max(s, axis=-1, keepdims=True))
        p = (e * (1.0 / jnp.sum(e, axis=-1, keepdims=True))).astype(jnp.bfloat16)
        o = jnp.dot(p, v, preferred_element_type=jnp.float32)
        for u in pair:
            for n, h in enumerate(heads):
                at = (u * stack + n) * nq
                part = o[at : at + nq, u * CH : (u + 1) * CH]
                mixed[u] = jnp.where(head_of == h, part, mixed[u])
    for u in pair:
        gated = (mixed[u] * picked(gate_ref, u)).astype(jnp.bfloat16)
        y = jnp.dot(gated, wo_ref[...], preferred_element_type=jnp.float32) + ob_ref[...]
        y = (picked(xq_ref, u).astype(jnp.float32) + y).astype(jnp.bfloat16)
        for b in range(nblk):
            part = y[b * block : (b + 1) * block]
            if len(out_ref.shape) == 4:
                out_ref[b, u] = part
            else:
                out_ref[u, pl.ds(starts[b], block), :] = part
        at = 0
        for ref in done_refs:
            for b in range(ref.shape[0]):
                t = pl.multiple_of(done_blk_ref[at] * block, 16)
                out_ref[u, pl.ds(t, block), :] = ref[b, u]
                at += 1
        if nnext:
            normed = normalize(out_ref[u], next_refs[0][...])
            next_out[0][u] = lax.dot_general(
                next_refs[1][...], normed, NT, preferred_element_type=jnp.float32
            ).astype(jnp.bfloat16)


def attend(ids, parts, xq, biases, wo, ob, done_ids, done, whole_out, stack, following):
    nrow, _, keys = parts[0].shape
    nblk = len(biases)
    nq = nblk * biases[0].shape[1] // 2 // HEADS
    shape = xq.shape if whole_out else (nblk, nrow, nq // nblk, CH)
    out = [jax.ShapeDtypeStruct(shape, jnp.bfloat16)]
    out_specs = [by_pair(out[0]) if whole_out else by_block(out[0])]
    if following:
        out.append(jax.ShapeDtypeStruct((nrow, 16, xq.shape[1]), jnp.bfloat16))
        out_specs.append(by_pair(out[1]))
    small = [wo, ob[None]]
    return pl.pallas_call(
        functools.partial(attention_kernel, nblk, len(done), stack, len(following)),
        grid_spec=pltpu.PrefetchScalarGridSpec(
            num_scalar_prefetch=2,
            grid=(nrow // 2,),
            in_specs=[by_pair(a) for a in parts]
            + [by_pair(xq)]
            + [whole(a) for a in list(biases) + small]
            + [by_block(a) for a in done]
            + [whole(a) for a in following],
            out_specs=out_specs,
            scratch_shapes=[pltpu.VMEM((HEADS * nq, keys), jnp.float32)],
        ),
        out_shape=out,
        compiler_params=pltpu.CompilerParams(vmem_limit_bytes=40 << 20),
        cost_estimate=pl.CostEstimate(
            flops=nblk * 28 * 10**8, bytes_accessed=6 << 20, transcendentals=nrow * HEADS * nq * keys
        ),
        name="attend",
    )(ids, done_ids, *parts, xq, *biases, *small, *done, *following)


def attention(ids, parts, xq, biases, wo, ob, following):
    done, at = [], 0
    for n in CALLS:
        last = at + n == len(biases)
        out = attend(
            ids[at : at + n],
            parts,
            xq,
            biases[at : at + n],
            wo,
            ob,
            ids[: max(at, 1)],
            done if last else [],
            last,
            1 if n > 2 else 2,
            following if last else [],
        )
        done.append(out[0])
        at += n
    return out


def solution(mesh):
    nr, nc = mesh.shape["row"], mesh.shape["col"]
    ng = nc // 2
    same_core_col = [[2 * g + c for g in range(ng)] for c in range(2)]
    same_core_all = [[r * nc + 2 * g + c for r in range(nr) for g in range(ng)] for c in range(2)]
    swap_core = [(i, i ^ 1) for i in range(nc)]
    ny = nr // 2
    across = [(r * nc + c, (r + ny) % nr * nc + (c ^ ng)) for r in range(nr) for c in range(nc)]

    def along_y(block, dy):
        return lax.ppermute(
            block, "row", [(i, i // ny * ny + (i + dy) % ny) for i in range(nr)]
        )

    def to_neighbour(block):
        return lax.ppermute(block, ("row", "col"), across)

    def spread(bias):
        return [along_y(bias, 1), along_y(bias, 3), to_neighbour(bias), along_y(bias, 2)]

    def spread_on(bias, first, parts):
        near, far, over, two = first
        over, two, parts = lax.optimization_barrier((over, two, parts))
        got = [bias, over, two, near, far, along_y(over, 1), along_y(over, 3), to_neighbour(two)]
        x, y = lax.axis_index("row") // ny, lax.axis_index("row") % ny
        turns = ((0, 0), (1, 0), (0, 2), (0, 1), (0, 3), (1, 1), (1, 3), (1, 2))
        ids = [(x ^ dx) * ny + (y + ny - dy) % ny for dx, dy in turns]
        return got, jnp.stack(ids).astype(jnp.int32), parts

    def all_to_all_16(message):
        return lax.all_to_all(
            message, "col", 0, 0, tiled=True, axis_index_groups=same_core_col
        )

    def per_device(pair, norm_gain, w_proj, w_bias, gate_bias, w_out, out_bias):
        core = lax.axis_index("col") % 2
        nrow = pair.shape[0] // ng
        ncol = pair.shape[1]
        keys = nc * ncol
        half = keys // 2
        normed = normalize(pair, norm_gain[0])
        local = jnp.einsum("qmc,ch->mhq", normed, w_bias[0], preferred_element_type=jnp.float32)
        local = local.astype(jnp.bfloat16).reshape(ncol, HEADS, 2, 2, ncol).transpose(0, 3, 1, 2, 4)
        local = local.reshape(ncol, 2, -1)
        own = jnp.where(core == 0, local[:, 0], local[:, 1])
        other = jnp.where(core == 0, local[:, 1], local[:, 0])
        other = lax.ppermute(other, "col", swap_core)
        local = jnp.concatenate([own, other], axis=1).reshape(-1, CH)
        brow = local.shape[0]
        message = jnp.broadcast_to(local[None], (ng,) + local.shape)
        message = jnp.concatenate([pair.reshape(ng, nrow * ncol, CH), message], axis=1)
        got = all_to_all_16(message)
        x_own = got[:, : nrow * ncol]
        x_other = lax.ppermute(x_own, "col", swap_core)
        bias = got[:, nrow * ncol :].reshape(half, half)
        first_biases = spread(bias)
        x = jnp.stack([x_own, x_other]).reshape(2, ng, nrow, ncol, CH)
        x = x.transpose(2, 0, 1, 3, 4).reshape(nrow, keys, CH)
        following = [norm_gain[1][None], jnp.pad(w_bias[1].T, ((0, 16 - HEADS), (0, 0)))]
        xq = x[:, :half]
        parts = prepare(x, xq, norm_gain[0], w_proj[0], gate_bias[0])
        biases, ids, parts = spread_on(bias, first_biases, parts)
        first, local = attention(ids, parts, xq, biases, w_out[0], out_bias[0], following)

        part = ncol // nr
        moved = first.reshape(nrow, ng, nr, part, CH).transpose(2, 1, 0, 3, 4)
        moved = moved.reshape(nr, ng, nrow * part, CH)
        local = local[:, :HEADS].reshape(nrow, HEADS, nr, half // nr).transpose(2, 0, 1, 3)
        local = local.reshape(nr, 1, -1, CH)
        brow = local.shape[2]
        message = jnp.concatenate(
            [
                moved,
                jnp.broadcast_to(local, (nr, ng, brow, CH)),
                jnp.zeros((nr, ng, -(brow + nrow * part) % 16, CH), jnp.bfloat16),
            ],
            axis=2,
        ).reshape(nr * ng, -1, CH)
        got = lax.all_to_all(
            message, ("row", "col"), 0, 0, tiled=True, axis_index_groups=same_core_all
        )
        x_own = got[:, : nrow * part].reshape(keys, part, CH).transpose(1, 0, 2)
        x_other = lax.ppermute(x_own, "col", swap_core)
        bias = got[:, nrow * part : nrow * part + brow].reshape(2, half, half // 2)
        bias = jnp.concatenate([bias[0], bias[1]], axis=1)
        first_biases = spread(bias)
        x = jnp.concatenate([x_own, x_other])
        xq = x.reshape(2 * part, ng, 2, ncol, CH)
        xq = jnp.where(core == 0, xq[:, :, 0], xq[:, :, 1]).reshape(2 * part, half, CH)
        parts = prepare(x, xq, norm_gain[1], w_proj[1], gate_bias[1])
        biases, ids, parts = spread_on(bias, first_biases, parts)
        (last,) = attention(ids, parts, xq, biases, w_out[1], out_bias[1], [])

        own = last[:part]
        other = lax.ppermute(last[part:], "col", swap_core)
        both = jnp.stack([jnp.where(core == 0, own, other), jnp.where(core == 0, other, own)])
        both = both.reshape(2, part, nr, half // nr, CH).transpose(2, 0, 1, 3, 4)
        got = lax.all_to_all(both.reshape(nr, -1, CH), "row", 0, 0, tiled=True)
        got = got.reshape(nr, 2, part, 2, ncol, CH)
        return got.transpose(3, 1, 4, 0, 2, 5).reshape(pair.shape)

    return jax.shard_map(
        per_device,
        mesh=mesh,
        in_specs=(P("row", "col", None), P(), P(), P(), P(), P(), P()),
        out_specs=P("row", "col", None),
        check_vma=False,
    )
```

```python
import functools

import jax
import jax.numpy as jnp
from jax import lax
from jax.experimental import pallas as pl
from jax.experimental.pallas import tpu as pltpu
from jax.sharding import PartitionSpec as P

HEADS = 4
WIDTH = 32
CH = 128
LOG2E = 1.4426950408889634
CALLS = (3, 5)
NT = (((1,), (1,)), ((), ()))


def normalize(values, gain):
    values = values.astype(jnp.float32)
    center = jnp.mean(values, axis=-1, keepdims=True)
    spread = jnp.mean((values - center) ** 2, axis=-1, keepdims=True)
    return ((values - center) * lax.rsqrt(spread + 1e-05) * gain).astype(jnp.bfloat16)


def normalize_once(values, gain):
    values = values.astype(jnp.float32)
    moved = values - values[..., :1]
    center = jnp.mean(moved, axis=-1, keepdims=True)
    spread = jnp.maximum(jnp.mean(moved * moved, axis=-1, keepdims=True) - center * center, 0.0)
    return ((moved - center) * lax.rsqrt(spread + 1e-05) * gain).astype(jnp.bfloat16)


def whole(a):
    return pl.BlockSpec(a.shape, lambda i, *_: (0,) * a.ndim)


def by_row(a):
    return pl.BlockSpec((1,) + a.shape[1:], lambda i, *_: (i, 0, 0))


def by_pair(a):
    return pl.BlockSpec((2,) + a.shape[1:], lambda i, *_: (i, 0, 0))


def by_block(a):
    return pl.BlockSpec((a.shape[0], 2) + a.shape[2:], lambda i, *_: (0, i, 0, 0))


def prepare_kernel(x_ref, xq_ref, gain_ref, wp_ref, gb_ref, kt_ref, v_ref, q_ref, gate_ref):
    gain = gain_ref[...]
    xn = normalize(x_ref[0], gain)
    k = jnp.dot(xn, wp_ref[:, CH : 2 * CH], preferred_element_type=jnp.float32)
    kt_ref[0] = k.astype(jnp.bfloat16).T
    v = jnp.dot(xn, wp_ref[:, 2 * CH : 3 * CH], preferred_element_type=jnp.float32)
    v_ref[0] = v.astype(jnp.bfloat16)
    xqn = normalize(xq_ref[0], gain)
    q = jnp.dot(xqn, wp_ref[:, :CH], preferred_element_type=jnp.float32)
    q_ref[0] = q.astype(jnp.bfloat16)
    gate = jnp.dot(xqn, wp_ref[:, 3 * CH :], preferred_element_type=jnp.float32)
    gate_ref[0] = jax.nn.sigmoid(gate + gb_ref[...])


def prepare(x, xq, gain, wp, gb):
    nrow, keys, _ = x.shape
    nq = xq.shape[1]
    outs = [
        jax.ShapeDtypeStruct((nrow, CH, keys), jnp.bfloat16),
        jax.ShapeDtypeStruct((nrow, keys, CH), jnp.bfloat16),
        jax.ShapeDtypeStruct((nrow, nq, CH), jnp.bfloat16),
        jax.ShapeDtypeStruct((nrow, nq, CH), jnp.float32),
    ]
    small = [gain[None], wp, gb[None]]
    return pl.pallas_call(
        prepare_kernel,
        grid=(nrow,),
        in_specs=[by_row(x), by_row(xq)] + [whole(a) for a in small],
        out_specs=[by_row(a) for a in outs],
        out_shape=outs,
        compiler_params=pltpu.CompilerParams(vmem_limit_bytes=16 << 20),
        cost_estimate=pl.CostEstimate(
            flops=4 * 10**9, bytes_accessed=6 << 20, transcendentals=nrow * nq * CH
        ),
        name="prepare",
    )(x, xq, *small)


def attention_kernel(nblk, ndone, stack, nnext, blk_ref, done_blk_ref, kt_ref, v_ref, q_ref, gate_ref, xq_ref, *refs):
    bias_refs = refs[:nblk]
    wo_ref, ob_ref = refs[nblk : nblk + 2]
    done_refs = refs[nblk + 2 : nblk + 2 + ndone]
    next_refs = refs[nblk + 2 + ndone : nblk + 2 + ndone + nnext]
    out_ref, *next_out, biasf = refs[nblk + 2 + ndone + nnext :]
    half = bias_refs[0].shape[0]
    rows = bias_refs[0].shape[1] // 2
    block = rows // HEADS
    nq = nblk * block

    @pl.when(pl.program_id(0) == 0)
    def _():
        for b in range(nblk):
            part = bias_refs[b][...].astype(jnp.float32).T * LOG2E
            for s in range(2):
                for h in range(HEADS):
                    at = s * rows + h * block
                    biasf[pl.ds(h * nq + b * block, block), pl.ds(s * half, half)] = part[
                        at : at + block
                    ]

    pair = range(2)
    kt = jnp.concatenate([kt_ref[u] for u in pair], axis=0)
    v = jnp.concatenate([v_ref[u] for u in pair], axis=1)
    starts = [pl.multiple_of(blk_ref[b] * block, 16) for b in range(nblk)]

    def picked(ref, u):
        return jnp.concatenate([ref[u, pl.ds(t, block), :] for t in starts], axis=0)

    q = [picked(q_ref, u) for u in pair]
    head_of = lax.broadcasted_iota(jnp.int32, q[0].shape, 1) // WIDTH
    zero = jnp.zeros_like(q[0])
    mixed = [jnp.zeros(q[0].shape, jnp.float32) for _ in pair]
    for h0 in range(0, HEADS, stack):
        heads = range(h0, h0 + stack)
        here = [jnp.where(head_of == h, q[0], zero) for h in heads]
        there = [jnp.where(head_of == h, q[1], zero) for h in heads]
        qh = jnp.concatenate(
            [jnp.concatenate([t, zero], axis=1) for t in here]
            + [jnp.concatenate([zero, t], axis=1) for t in there],
            axis=0,
        )
        s = jnp.dot(qh, kt, preferred_element_type=jnp.float32)
        bias = biasf[h0 * nq : (h0 + stack) * nq]
        s = s * (WIDTH**-0.5 * LOG2E) + jnp.concatenate([bias, bias], axis=0)
        e = jnp.exp2(s - jnp.max(s, axis=-1, keepdims=True))
        p = (e * (1.0 / jnp.sum(e, axis=-1, keepdims=True))).astype(jnp.bfloat16)
        o = jnp.dot(p, v, preferred_element_type=jnp.float32)
        for u in pair:
            for n, h in enumerate(heads):
                at = (u * stack + n) * nq
                part = o[at : at + nq, u * CH : (u + 1) * CH]
                mixed[u] = jnp.where(head_of == h, part, mixed[u])
    for u in pair:
        gated = (mixed[u] * picked(gate_ref, u)).astype(jnp.bfloat16)
        y = jnp.dot(gated, wo_ref[...], preferred_element_type=jnp.float32) + ob_ref[...]
        y = (picked(xq_ref, u).astype(jnp.float32) + y).astype(jnp.bfloat16)
        for b in range(nblk):
            part = y[b * block : (b + 1) * block]
            if len(out_ref.shape) == 4:
                out_ref[b, u] = part
            else:
                out_ref[u, pl.ds(starts[b], block), :] = part
        at = 0
        for ref in done_refs:
            for b in range(ref.shape[0]):
                t = pl.multiple_of(done_blk_ref[at] * block, 16)
                out_ref[u, pl.ds(t, block), :] = ref[b, u]
                at += 1
        if nnext:
            normed = normalize(out_ref[u], next_refs[0][...])
            next_out[0][u] = lax.dot_general(
                next_refs[1][...], normed, NT, preferred_element_type=jnp.float32
            ).astype(jnp.bfloat16)


def attend(ids, parts, xq, biases, wo, ob, done_ids, done, whole_out, stack, following):
    nrow, _, keys = parts[0].shape
    nblk = len(biases)
    nq = nblk * biases[0].shape[1] // 2 // HEADS
    shape = xq.shape if whole_out else (nblk, nrow, nq // nblk, CH)
    out = [jax.ShapeDtypeStruct(shape, jnp.bfloat16)]
    out_specs = [by_pair(out[0]) if whole_out else by_block(out[0])]
    if following:
        out.append(jax.ShapeDtypeStruct((nrow, 16, xq.shape[1]), jnp.bfloat16))
        out_specs.append(by_pair(out[1]))
    small = [wo, ob[None]]
    return pl.pallas_call(
        functools.partial(attention_kernel, nblk, len(done), stack, len(following)),
        grid_spec=pltpu.PrefetchScalarGridSpec(
            num_scalar_prefetch=2,
            grid=(nrow // 2,),
            in_specs=[by_pair(a) for a in parts]
            + [by_pair(xq)]
            + [whole(a) for a in list(biases) + small]
            + [by_block(a) for a in done]
            + [whole(a) for a in following],
            out_specs=out_specs,
            scratch_shapes=[pltpu.VMEM((HEADS * nq, keys), jnp.float32)],
        ),
        out_shape=out,
        compiler_params=pltpu.CompilerParams(vmem_limit_bytes=40 << 20),
        cost_estimate=pl.CostEstimate(
            flops=nblk * 28 * 10**8, bytes_accessed=6 << 20, transcendentals=nrow * HEADS * nq * keys
        ),
        name="attend",
    )(ids, done_ids, *parts, xq, *biases, *small, *done, *following)


def attention(ids, parts, xq, biases, wo, ob, following):
    done, at = [], 0
    for n in CALLS:
        last = at + n == len(biases)
        out = attend(
            ids[at : at + n],
            parts,
            xq,
            biases[at : at + n],
            wo,
            ob,
            ids[: max(at, 1)],
            done if last else [],
            last,
            1 if n > 2 else 2,
            following if last else [],
        )
        done.append(out[0])
        at += n
    return out


def solution(mesh):
    nr, nc = mesh.shape["row"], mesh.shape["col"]
    ng = nc // 2
    same_core_col = [[2 * g + c for g in range(ng)] for c in range(2)]
    same_core_all = [[r * nc + 2 * g + c for r in range(nr) for g in range(ng)] for c in range(2)]
    swap_core = [(i, i ^ 1) for i in range(nc)]
    ny = nr // 2
    across = [(r * nc + c, (r + ny) % nr * nc + (c ^ ng)) for r in range(nr) for c in range(nc)]

    def along_y(block, dy):
        return lax.ppermute(
            block, "row", [(i, i // ny * ny + (i + dy) % ny) for i in range(nr)]
        )

    def to_neighbour(block):
        return lax.ppermute(block, ("row", "col"), across)

    def spread(bias):
        return [along_y(bias, 1), along_y(bias, 3), to_neighbour(bias), along_y(bias, 2)]

    def spread_on(bias, first, parts):
        near, far, over, two = first
        over, two, parts = lax.optimization_barrier((over, two, parts))
        got = [bias, over, two, near, far, along_y(over, 1), along_y(over, 3), to_neighbour(two)]
        x, y = lax.axis_index("row") // ny, lax.axis_index("row") % ny
        turns = ((0, 0), (1, 0), (0, 2), (0, 1), (0, 3), (1, 1), (1, 3), (1, 2))
        ids = [(x ^ dx) * ny + (y + ny - dy) % ny for dx, dy in turns]
        return got, jnp.stack(ids).astype(jnp.int32), parts

    def all_to_all_16(message):
        return lax.all_to_all(
            message, "col", 0, 0, tiled=True, axis_index_groups=same_core_col
        )

    def per_device(pair, norm_gain, w_proj, w_bias, gate_bias, w_out, out_bias):
        core = lax.axis_index("col") % 2
        nrow = pair.shape[0] // ng
        ncol = pair.shape[1]
        keys = nc * ncol
        half = keys // 2
        normed = normalize_once(pair, norm_gain[0])
        local = jnp.einsum("qmc,ch->mhq", normed, w_bias[0], preferred_element_type=jnp.float32)
        local = local.astype(jnp.bfloat16).reshape(ncol, HEADS, 2, 2, ncol).transpose(0, 3, 1, 2, 4)
        local = local.reshape(ncol, 2, -1)
        own = jnp.where(core == 0, local[:, 0], local[:, 1])
        other = jnp.where(core == 0, local[:, 1], local[:, 0])
        other = lax.ppermute(other, "col", swap_core)
        local = jnp.concatenate([own, other], axis=1).reshape(-1, CH)
        brow = local.shape[0]
        message = jnp.broadcast_to(local[None], (ng,) + local.shape)
        message = jnp.concatenate([pair.reshape(ng, nrow * ncol, CH), message], axis=1)
        got = all_to_all_16(message)
        x_own = got[:, : nrow * ncol]
        x_other = lax.ppermute(x_own, "col", swap_core)
        bias = got[:, nrow * ncol :].reshape(half, half)
        first_biases = spread(bias)
        x = jnp.stack([x_own, x_other]).reshape(2, ng, nrow, ncol, CH)
        x = x.transpose(2, 0, 1, 3, 4).reshape(nrow, keys, CH)
        following = [norm_gain[1][None], jnp.pad(w_bias[1].T, ((0, 16 - HEADS), (0, 0)))]
        xq = x[:, :half]
        parts = prepare(x, xq, norm_gain[0], w_proj[0], gate_bias[0])
        biases, ids, parts = spread_on(bias, first_biases, parts)
        first, local = attention(ids, parts, xq, biases, w_out[0], out_bias[0], following)

        part = ncol // nr
        moved = first.reshape(nrow, ng, nr, part, CH).transpose(2, 1, 0, 3, 4)
        moved = moved.reshape(nr, ng, nrow * part, CH)
        local = local[:, :HEADS].reshape(nrow, HEADS, nr, half // nr).transpose(2, 0, 1, 3)
        local = local.reshape(nr, 1, -1, CH)
        brow = local.shape[2]
        message = jnp.concatenate(
            [
                moved,
                jnp.broadcast_to(local, (nr, ng, brow, CH)),
                jnp.zeros((nr, ng, -(brow + nrow * part) % 16, CH), jnp.bfloat16),
            ],
            axis=2,
        ).reshape(nr * ng, -1, CH)
        got = lax.all_to_all(
            message, ("row", "col"), 0, 0, tiled=True, axis_index_groups=same_core_all
        )
        bias = got[:, nrow * part : nrow * part + brow].reshape(2, half, half // 2)
        bias = jnp.concatenate([bias[0], bias[1]], axis=1)
        got, bias = lax.optimization_barrier((got, bias))
        first_biases = spread(bias)
        x_own = got[:, : nrow * part].reshape(keys, part, CH).transpose(1, 0, 2)
        x_other = lax.ppermute(x_own, "col", swap_core)
        x = jnp.concatenate([x_own, x_other])
        xq = x.reshape(2 * part, ng, 2, ncol, CH)
        xq = jnp.where(core == 0, xq[:, :, 0], xq[:, :, 1]).reshape(2 * part, half, CH)
        parts = prepare(x, xq, norm_gain[1], w_proj[1], gate_bias[1])
        biases, ids, parts = spread_on(bias, first_biases, parts)
        (last,) = attention(ids, parts, xq, biases, w_out[1], out_bias[1], [])

        own = last[:part]
        other = lax.ppermute(last[part:], "col", swap_core)
        both = jnp.stack([jnp.where(core == 0, own, other), jnp.where(core == 0, other, own)])
        both = both.reshape(2, part, nr, half // nr, CH).transpose(2, 0, 1, 3, 4)
        got = lax.all_to_all(both.reshape(nr, -1, CH), "row", 0, 0, tiled=True)
        got = got.reshape(nr, 2, part, 2, ncol, CH)
        return got.transpose(3, 1, 4, 0, 2, 5).reshape(pair.shape)

    return jax.shard_map(
        per_device,
        mesh=mesh,
        in_specs=(P("row", "col", None), P(), P(), P(), P(), P(), P()),
        out_specs=P("row", "col", None),
        check_vma=False,
    )
```
